128 devices in a mesh: lat: 8 (over x_lo, y), lon: 16 (over z, x_hi, core).
Axes of the slice: x: 4 (x_hi: 2, x_lo: 2; x = x_hi * 2 + x_lo), y: 4, z: 4, core: 2. Of those that a mesh axis runs over, the one named last changes fastest.
Arguments:
- sensitivity: float32 [3, 3, 2880, 5760], P(None, None, 'lat', 'lon'), may hold values from -6 to 6
- zonal_courant: float32 [2, 3, 2880, 5760], P(None, None, 'lat', 'lon'), may hold values from -0.45 to 0.45
- merid_courant: float32 [2, 3, 2880, 5760], P(None, None, 'lat', 'lon'), may hold values from -0.45 to 0.45
Outputs:
- adjoint: float32 [3, 3, 2880, 5760], P(None, None, 'lat', 'lon')
The draws below stay inside these ranges and needn't reach their ends.
All inputs are finite; a program needn't handle non-finite values.
Results may differ from the reference program's by a relative error of at most 0.0003.
Values sent between devices are 32-bit elements; how exact they have to be, the bound alone decides.
No kernel may reach another device: no remote copies, remote signals or barrier semaphores. Data moves between devices by JAX's collectives and lax.ppermute only.
A program may use at most 128 MiB of HBM per device.

```python
import jax
import jax.numpy as jnp
from jax import lax

LEVELS = 3
TRACERS = 3
STEPS = 2
NLAT = 2880
NLON = 5760


def steps_of(own_key, extent, cuts, low, top_value):
    factor_of = 1.0
    for axis_at, parts in cuts:
        draws = jax.random.uniform(jax.random.fold_in(jax.random.fold_in(own_key, 6), axis_at), (parts,), jnp.float32, low / len(cuts), top_value / len(cuts))
        factor_of = factor_of * jnp.repeat(jnp.exp(draws), extent[axis_at] // parts).reshape((-1,) + (1,) * (len(extent) - 1 - axis_at))
    return factor_of


def normal_values(own_key, extent, deviation, reach, shards=(), kind=jnp.bfloat16):
    gain = steps_of(own_key, extent, shards, -0.22, 0.18) if shards else 1.0
    drawn = jax.random.normal(own_key, extent, jnp.float32) * deviation * gain
    return jnp.minimum(jnp.maximum(drawn, -reach), reach).astype(kind)


def setup_inputs(seed: int = 0) -> dict:
    arg_keys = jax.random.split(jax.random.key(seed), 4)
    return {
        "sensitivity": normal_values(arg_keys[0], (TRACERS, LEVELS, NLAT, NLON), 1.0, 6.0, ((2, 8), (3, 16)), jnp.float32),
        "zonal_courant": jnp.clip(jax.random.uniform(arg_keys[1], (STEPS, LEVELS, NLAT, NLON), jnp.float32, -0.45, 0.45) * steps_of(arg_keys[1], (STEPS, LEVELS, NLAT, NLON), ((2, 8), (3, 16)), -0.4, 0.0), -0.45, 0.45),
        "merid_courant": jnp.clip(jax.random.uniform(arg_keys[2], (STEPS, LEVELS, NLAT, NLON), jnp.float32, -0.45, 0.45) * steps_of(arg_keys[2], (STEPS, LEVELS, NLAT, NLON), ((2, 8), (3, 16)), -0.4, 0.0), -0.45, 0.45),
    }


def face_flux(field_in, courant, axis_dim):
    length = field_in.shape[axis_dim]

    def part_of(start_at, stop_at):
        return lax.slice_in_dim(field_in, start_at, stop_at, axis=axis_dim)
    face_vals = 7.0 / 12.0 * (part_of(1, length - 2) + part_of(2, length - 1)) - 1.0 / 12.0 * (part_of(0, length - 3) + part_of(3, length))
    west_val = lax.slice_in_dim(face_vals, 0, length - 4, axis=axis_dim)
    east_val = lax.slice_in_dim(face_vals, 1, length - 3, axis=axis_dim)
    centre = part_of(2, length - 2)
    slope_all = east_val - west_val
    curve_all = 6.0 * centre - 3.0 * (west_val + east_val)

    def lower_cell(values):
        return lax.slice_in_dim(values, 0, length - 5, axis=axis_dim)

    def upper_cell(values):
        return lax.slice_in_dim(values, 1, length - 4, axis=axis_dim)
    from_west = lower_cell(east_val) - 0.5 * courant * (lower_cell(slope_all) - (1.0 - courant * (2.0 / 3.0)) * lower_cell(curve_all))
    from_east = upper_cell(west_val) - 0.5 * courant * (upper_cell(slope_all) + (1.0 + courant * (2.0 / 3.0)) * upper_cell(curve_all))
    return courant * jnp.where(courant > 0, from_west, from_east)

def transport(tracer, wind_pair, row_first, lat_total):
    zonal_cell = wind_pair[0]
    merid_cell = wind_pair[1]
    face_zonal = 0.5 * (zonal_cell[:, 1:-1, :-1] + zonal_cell[:, 1:-1, 1:])
    face_merid = 0.5 * (merid_cell[:, :-1, 1:-1] + merid_cell[:, 1:, 1:-1])
    flux_zonal = face_flux(tracer[:, :, 3:-3, :], face_zonal[None], 3)
    flux_merid = face_flux(tracer[:, :, :, 3:-3], face_merid[None], 2)
    rows_out = flux_zonal.shape[2]
    face_rows = row_first + jnp.arange(rows_out + 1, dtype=jnp.int32)
    face_angle = jnp.pi * face_rows.astype(jnp.float32) / lat_total
    face_metric = jnp.where(face_rows % lat_total == 0, 0.0, jnp.abs(jnp.sin(face_angle)))
    cell_metric = jnp.abs(jnp.sin(jnp.pi * (face_rows[:-1].astype(jnp.float32) + 0.5) / lat_total))
    zonal_part = flux_zonal[..., 1:] - flux_zonal[..., :-1]
    merid_part = (face_metric[1:, None] * flux_merid[:, :, 1:, :] - face_metric[:-1, None] * flux_merid[:, :, :-1, :]) / cell_metric[:, None]
    return tracer[:, :, 3:-3, 3:-3] - zonal_part - merid_part

def polar_pad(field_in, rim_depth):
    half_turn = field_in.shape[-1] // 2
    turned = jnp.roll(field_in, half_turn, axis=-1)
    south_rows = jnp.flip(turned[..., :rim_depth, :], axis=-2)
    north_rows = jnp.flip(turned[..., -rim_depth:, :], axis=-2)
    return jnp.concatenate([south_rows, field_in, north_rows], axis=-2)

def reference(sensitivity, zonal_courant, merid_courant):
    lat_total = sensitivity.shape[2]
    adjoint = sensitivity
    for step_index in range(STEPS - 1, -1, -1):
        wind_pair = jnp.stack([zonal_courant[step_index], merid_courant[step_index]])
        wind_pair = jnp.pad(wind_pair, ((0, 0), (0, 0), (1, 1), (0, 0)))
        wind_pair = jnp.concatenate([wind_pair[..., -1:], wind_pair, wind_pair[..., :1]], axis=-1)

        def one_tracer(cotangent):

            def forward(tracer):
                padded = polar_pad(tracer, 3)
                padded = jnp.concatenate([padded[..., -3:], padded, padded[..., :3]], axis=-1)
                return transport(padded[None], wind_pair, 0, lat_total)[0]
            primal, pullback = jax.vjp(forward, jnp.zeros_like(cotangent))
            return pullback(cotangent)[0]
        adjoint = lax.map(one_tracer, adjoint)
    return adjoint
```

```python
import jax
import jax.numpy as jnp
import numpy as np
from jax import lax
from jax.experimental import pallas as pl
from jax.experimental.pallas import tpu as pltpu
from jax.sharding import PartitionSpec as P

N = 360
LANES = 384
HALO = 6
ROWS = N // 8
FRONT = 8
PADDED = 376
F32 = jnp.float32
BF16 = jnp.bfloat16
AXES = ("lat", "lon")


def params(**kw):
    return pltpu.CompilerParams(vmem_limit_bytes=56 * 2**20, **kw)


def lam_base(level, tracer):
    return 6 * (3 * level + tracer)


def z1_base(level):
    return 54 + 6 * level


def m1_base(level):
    return 72 + 3 * level


def z0_base(level):
    return 81 + 3 * level


def pack_columns(sw_ref, se_ref, zw_ref, ze_ref, mw_ref, me_ref, left_ref, right_ref, east_s, west_s):
    level = pl.program_id(0)
    odd = lax.axis_index("lon") % 2
    jobs = [(sw_ref, se_ref, t, HALO, lam_base(level, t)) for t in range(3)]
    jobs.append((zw_ref, ze_ref, 1, HALO, z1_base(level)))
    jobs.append((mw_ref, me_ref, 0, 3, m1_base(level)))
    jobs.append((zw_ref, ze_ref, 0, 3, z0_base(level)))

    @pl.when(level == 0)
    def _():
        east_s[...] = jnp.zeros((N, 128), F32)
        west_s[...] = jnp.zeros((N, 128), F32)

    lane = lax.broadcasted_iota(jnp.int32, (ROWS, 128), 1)
    chunk = 72
    lane = lax.broadcasted_iota(jnp.int32, (chunk, 128), 1)

    def body(r, _):
        rows = pl.ds(r * chunk, chunk)
        east = east_s[rows, :]
        west = west_s[rows, :]
        for w_ref, e_ref, k, width, base in jobs:
            both = jnp.where(lane < 64, w_ref[k, 0, rows, :], e_ref[k, 0, rows, :])
            shift = lax.rem(base + 30 - (HALO - width) + 128, 128)
            turned_e = pltpu.roll(both, shift, 1)
            turned_w = turned_e if width == HALO else pltpu.roll(both, base + 30, 1)
            east = jnp.where((lane >= base) & (lane < base + width), turned_e, east)
            west = jnp.where((lane >= base + 30) & (lane < base + 30 + width), turned_w, west)
        east_s[rows, :] = east
        west_s[rows, :] = west

        @pl.when(level == 2)
        def _():
            is_odd = (jnp.zeros((chunk, 128), jnp.int32) + odd) == 1
            left_ref[rows, :] = jnp.where(is_odd, west, east)
            right_ref[rows, :] = jnp.where(is_odd, east, west)

        return 0

    lax.fori_loop(0, N // chunk, body, 0)


def make_columns_message(sens, zonal, merid):
    def spec(lead, step, tile):
        return pl.BlockSpec((lead, 1, N, 128), lambda l: (step, l, 0, tile))

    whole = pl.BlockSpec((N, 128), lambda l: (0, 0))
    shape = jax.ShapeDtypeStruct((N, 128), F32)
    return pl.pallas_call(
        pack_columns,
        grid=(3,),
        in_specs=[spec(3, 0, 0), spec(3, 0, 2), spec(2, 0, 0), spec(2, 0, 2), spec(1, 1, 0), spec(1, 1, 2)],
        out_specs=[whole, whole],
        out_shape=[shape, shape],
        scratch_shapes=[pltpu.VMEM((N, 128), F32)] * 2,
        compiler_params=params(),
        name="pack_columns",
    )(sens, sens, zonal, zonal, merid, merid)


def with_halo(own, east_msg, west_msg, base, width, lane):
    from_west = pltpu.roll(west_msg, lax.rem(128 - width - base + 256, 128), 1)
    from_east = pltpu.roll(east_msg, lax.rem(104 - base - 30 + 256, 128), 1)
    return jnp.where(lane < 104, own, jnp.where(lane < 116, from_east, from_west))


def sorted_by_side(left, right, odd, shape):
    is_odd = (jnp.zeros(shape, jnp.int32) + odd) == 1
    return jnp.where(is_odd, right, left), jnp.where(is_odd, left, right)


def flipped(rows, count):
    return jnp.concatenate([rows[count - 1 - k : count - k] for k in range(count)], axis=0)


def pack_rows(ss_ref, sn_ref, zs_ref, zn_ref, ms_ref, mn_ref, ls_ref, ln_ref, rs_ref, rn_ref, a_ref, b_ref):
    level = pl.program_id(0)
    lat = lax.axis_index("lat")
    odd = lax.axis_index("lon") % 2
    lane = lax.broadcasted_iota(jnp.int32, (8, 128), 1)
    at_south = lat == 0
    at_north = lat == lax.axis_size("lat") - 1
    lat_odd = lat % 2
    for north in (False, True):
        s_ref, z_ref, m_ref = (sn_ref, zn_ref, mn_ref) if north else (ss_ref, zs_ref, ms_ref)
        l_ref, r_ref = (ln_ref, rn_ref) if north else (ls_ref, rs_ref)
        east_msg, west_msg = sorted_by_side(l_ref[...], r_ref[...], odd, (8, 128))
        pole = at_north if north else at_south
        turn = (jnp.zeros((8, 128), jnp.int32) + pole.astype(jnp.int32)) == 1
        slots = [(s_ref, t, HALO, HALO, lam_base(level, t), 6 * t, 1.0) for t in range(3)]
        slots.append((m_ref, 1, 6, 3, m1_base(level), 18, -1.0))
        slots.append((z_ref, 1, 3, HALO, z1_base(level), 24, 1.0))
        slots.append((m_ref, 0, 3, 0, 0, 27, -1.0))
        for ref, k, count, width, base, at, sign in slots:
            for tile in range(3):
                rows = ref[k, 0, :, tile * 128 : (tile + 1) * 128]
                if tile == 2:
                    if width:
                        rows = with_halo(rows, east_msg, west_msg, base, width, lane)
                    else:
                        rows = jnp.where(lane < 104, rows, 0.0)
                picked = rows[8 - count :] if north else rows[:count]
                picked = jnp.where(turn[:count], sign * flipped(picked, count), picked)
                cols = pl.ds(tile * 128, 128)
                if north:
                    @pl.when(lat_odd == 0)
                    def _():
                        a_ref[0, pl.ds(at, count), cols] = picked

                    @pl.when(lat_odd == 1)
                    def _():
                        b_ref[0, pl.ds(at, count), cols] = picked
                else:
                    @pl.when(lat_odd == 1)
                    def _():
                        a_ref[0, pl.ds(at, count), cols] = picked

                    @pl.when(lat_odd == 0)
                    def _():
                        b_ref[0, pl.ds(at, count), cols] = picked
    for out in (a_ref, b_ref):
        out[0, pl.ds(30, 2), :] = jnp.zeros((2, LANES), F32)


def make_rows_message(sens, zonal, merid, left, right):
    last = N // 8 - 1

    def spec(lead, block):
        return pl.BlockSpec((lead, 1, 8, LANES), lambda l: (0, l, block, 0))

    def msg(block):
        return pl.BlockSpec((8, 128), lambda l: (block, 0))

    out = pl.BlockSpec((1, 32, LANES), lambda l: (l, 0, 0))
    shape = jax.ShapeDtypeStruct((3, 32, LANES), F32)
    return pl.pallas_call(
        pack_rows,
        grid=(3,),
        in_specs=[spec(3, 0), spec(3, last), spec(2, 0), spec(2, last), spec(2, 0), spec(2, last)]
        + [msg(0), msg(last), msg(0), msg(last)],
        out_specs=[out, out],
        out_shape=[shape, shape],
        compiler_params=params(),
        name="pack_rows",
    )(sens, sens, zonal, zonal, merid, merid, left, left, right, right)


def permuted(values, table):
    high = values.astype(BF16)
    low = (values - high.astype(F32)).astype(BF16)
    return jnp.dot(jnp.concatenate([high, low], axis=1), table, preferred_element_type=F32)


def weights(total, scale):
    speed = jnp.abs(total) * 0.5
    lead = total * scale
    quad = lead * speed
    b = quad - quad * speed
    a = lead - quad - b
    c = (quad + b + b) * 12.0
    zero = jnp.zeros_like(b)
    return a, jnp.maximum(b, zero), jnp.minimum(b, zero), jnp.maximum(c, zero), jnp.minimum(c, zero)


def y_pass(load, wind, hinv, gface, store, first, last):
    scaled, faces, parts, eps, dee = {}, {}, {}, {}, {}

    def scaled_at(i):
        if i not in scaled:
            h = hinv(i)
            scaled[i] = [load(t, i) * h for t in range(3)]
        return scaled[i]

    def parts_at(f):
        if f not in parts:
            w = weights(wind(f - 1) + wind(f), gface(f))
            lo, hi = scaled_at(f - 1), scaled_at(f)
            phi = [hi[t] - lo[t] for t in range(3)]
            parts[f] = [[x * p for x in w] for p in phi]
        return parts[f]

    def eps_at(f):
        if f not in eps:
            p0, p1, pm = parts_at(f), parts_at(f + 1), parts_at(f - 1)
            eps[f] = [p0[t][0] - p1[t][1] - pm[t][2] for t in range(3)]
        return eps[f]

    def dee_at(i):
        if i not in dee:
            e0, e1 = eps_at(i), eps_at(i + 1)
            dee[i] = [e0[t] + e1[t] for t in range(3)]
        return dee[i]

    for i in range(first, last):
        dm, d0, dp = dee_at(i - 1), dee_at(i), dee_at(i + 1)
        p0, p1 = parts_at(i), parts_at(i + 1)
        for t in range(3):
            store(t, i, load(t, i) + (p0[t][4] + p1[t][3]) + (8.0 * d0[t] - (dm[t] + dp[t])))


def x_row(field, total, acc):
    w = [weights(total[p], 1.0 / 24.0) for p in range(3)]

    def one(f, base):
        phi = [f[0] - pltpu.roll(f[2], 1, 1), f[1] - f[0], f[2] - f[1]]
        a, bp, bm, cp, cm = [[w[p][k] * phi[p] for p in range(3)] for k in range(5)]
        e0 = a[0] - bp[1] - pltpu.roll(bm[2], 1, 1)
        e1 = a[1] - bp[2] - bm[0]
        e2 = a[2] - pltpu.roll(bp[0], 127, 1) - bm[1]
        s0, s1, s2 = 7.0 * e0, 7.0 * e1, 7.0 * e2
        out0 = (base[0] + cm[0]) + (cp[1] + s0) + (s1 - e2) - pltpu.roll(e2, 1, 1)
        out1 = (base[1] + cm[1]) + (cp[2] + s1) + (s2 - e0) - pltpu.roll(e0, 127, 1)
        out2 = (base[2] + cm[2]) + (s2 - e1) + pltpu.roll(cp[0] + (s0 - e1), 127, 1)
        return out0, out1, out2

    return [one(field[t], acc[t]) for t in range(3)]


def advance(
    s_ref, z_ref, m_ref, left_ref, right_ref, a_ref, b_ref, fwd_ref, inv_ref, h_ref, g_ref,
    out_ref, lam, zon, mer, acc, lam1, res,
):
    level = pl.program_id(0)
    lat_odd = lax.axis_index("lat") % 2
    lon_odd = lax.axis_index("lon") % 2
    chunk = 120
    lane = lax.broadcasted_iota(jnp.int32, (chunk, 128), 1)

    def take(r, _):
        rows = pl.ds(pl.multiple_of(r * chunk, 8), chunk)
        east_msg, west_msg = sorted_by_side(left_ref[rows, :], right_ref[rows, :], lon_odd, (chunk, 128))
        jobs = [(s_ref, t, HALO, lam_base(level, t), lam, t) for t in range(3)]
        jobs += [(z_ref, 1, HALO, z1_base(level), zon, 1), (z_ref, 0, 3, z0_base(level), zon, 0)]
        jobs += [(m_ref, 1, 3, m1_base(level), mer, 1), (m_ref, 0, 0, 0, mer, 0)]
        for ref, k, width, base, dst, j in jobs:
            tail = ref[k, 0, rows, 256:384]
            if width:
                tail = with_halo(tail, east_msg, west_msg, base, width, lane)
            else:
                tail = jnp.where(lane < 104, tail, 0.0)
            whole = jnp.concatenate([ref[k, 0, rows, 0:256], tail], axis=1)
            moved = permuted(whole, fwd_ref[...])
            for p in range(3):
                dst[j, p, pl.ds(pl.multiple_of(FRONT + r * chunk, 8), chunk), :] = moved[:, p * 128 : (p + 1) * 128]
        return 0

    lax.fori_loop(0, N // chunk, take, 0)

    got_a, got_b = permuted(a_ref[0], fwd_ref[...]), permuted(b_ref[0], fwd_ref[...])
    odd = (jnp.zeros((32, LANES), jnp.int32) + lat_odd) == 1
    north = jnp.where(odd, got_b, got_a)
    south = jnp.where(odd, got_a, got_b)
    slots = [(lam, t, 6, 6 * t) for t in range(3)]
    slots += [(mer, 1, 6, 18), (zon, 1, 3, 24), (mer, 0, 3, 27)]
    for dst, j, count, at in slots:
        for p in range(3):
            cols = slice(p * 128, (p + 1) * 128)
            dst[j, p, pl.ds(FRONT - count, count), :] = south[at : at + count, cols]
            dst[j, p, pl.ds(FRONT + N, count), :] = north[at : at + count, cols]

    def strip(ref, j, p, i):
        return ref[j, p, pl.ds(FRONT + i, 8, stride=ROWS), :]

    def hinv(i):
        return h_ref[i + 6]

    def gface(f):
        return g_ref[f + 6]

    def y_one(p, _):
        def store(t, i, value):
            acc[t, p, i + 3] = value

        y_pass(lambda t, i: strip(lam, t, p, i), lambda i: strip(mer, 1, p, i), hinv, gface, store, -3, ROWS + 3)
        return 0

    lax.fori_loop(0, 3, y_one, 0)

    def zonal_total(step, i):
        z = [strip(zon, step, p, i) for p in range(3)]
        return [z[0] + pltpu.roll(z[2], 1, 1), z[1] + z[0], z[2] + z[1]]

    def x_one(q, _):
        for k in range(3):
            i = 3 * q + k
            field = [[strip(lam, t, p, i - 3) for p in range(3)] for t in range(3)]
            base = [[acc[t, p, i] for p in range(3)] for t in range(3)]
            new = x_row(field, zonal_total(1, i - 3), base)
            for t in range(3):
                for p in range(3):
                    lam1[t, p, i] = new[t][p]
        return 0

    lax.fori_loop(0, (ROWS + 6) // 3, x_one, 0)

    def y_two(p, _):
        def store(t, i, value):
            acc[t, p, i] = value

        y_pass(lambda t, i: lam1[t, p, i + 3], lambda i: strip(mer, 0, p, i), hinv, gface, store, 0, ROWS)
        return 0

    lax.fori_loop(0, 3, y_two, 0)

    def x_two(q, _):
        for k in range(3):
            i = 3 * q + k
            field = [[lam1[t, p, i + 3] for p in range(3)] for t in range(3)]
            base = [[acc[t, p, i] for p in range(3)] for t in range(3)]
            new = x_row(field, zonal_total(0, i), base)
            for t in range(3):
                for p in range(3):
                    res[t, p, pl.ds(i, 8, stride=ROWS), :] = new[t][p]
        return 0

    lax.fori_loop(0, ROWS // 3, x_two, 0)

    def give(r, _):
        rows = pl.ds(pl.multiple_of(r * chunk, 8), chunk)
        for t in range(3):
            phases = jnp.concatenate([res[t, p, rows, :] for p in range(3)], axis=1)
            out_ref[t, 0, rows, :] = permuted(phases, inv_ref[...])
        return 0

    lax.fori_loop(0, N // chunk, give, 0)


def run_steps(sens, zonal, merid, left, right, a, b, hinv, gface):
    order = np.zeros((LANES, LANES), np.float32)
    for x in range(LANES):
        order[x, (x % 3) * 128 + x // 3] = 1.0
    fwd = jnp.asarray(np.concatenate([order, order]), BF16)
    inv = jnp.asarray(np.concatenate([order.T, order.T]), BF16)

    def block(lead):
        return pl.BlockSpec((lead, 1, N, LANES), lambda l: (0, l, 0, 0))

    def whole(shape):
        return pl.BlockSpec(shape, lambda l: (0,) * len(shape))

    rows_msg = pl.BlockSpec((1, 32, LANES), lambda l: (l, 0, 0))
    table = (ROWS + 12, 8, 128)
    return pl.pallas_call(
        advance,
        grid=(3,),
        in_specs=[block(3), block(2), block(2), whole((N, 128)), whole((N, 128)), rows_msg, rows_msg]
        + [whole((2 * LANES, LANES))] * 2 + [whole(table)] * 2,
        out_specs=block(3),
        out_shape=jax.ShapeDtypeStruct(sens.shape, F32),
        scratch_shapes=[
            pltpu.VMEM((3, 3, PADDED, 128), F32),
            pltpu.VMEM((2, 3, PADDED, 128), F32),
            pltpu.VMEM((2, 3, PADDED, 128), F32),
            pltpu.VMEM((3, 3, ROWS + 6, 8, 128), F32),
            pltpu.VMEM((3, 3, ROWS + 6, 8, 128), F32),
            pltpu.VMEM((3, 3, N, 128), F32),
        ],
        compiler_params=params(),
        name="advance",
    )(sens, zonal, merid, left, right, a, b, fwd, inv, hinv, gface)


def exchanges(lat_count, lon_count):
    def at(la, lo):
        return la * lon_count + lo % lon_count

    cells = [(la, lo) for la in range(lat_count) for lo in range(lon_count)]
    half = lon_count // 2
    left = [(at(la, lo), at(la, lo ^ 1)) for la, lo in cells]
    right = [(at(la, lo), at(la, lo + 1 if lo % 2 else lo - 1)) for la, lo in cells]
    a = [(at(la, lo), at(la ^ 1, lo)) for la, lo in cells]
    b = []
    for la, lo in cells:
        to = la + 1 if la % 2 else la - 1
        if to < 0 or to == lat_count:
            b.append((at(la, lo), at(la, lo + half)))
        else:
            b.append((at(la, lo), at(to, lo)))
    return left, right, a, b


def metric_tables(lat_total):
    first = lax.axis_index("lat") * N
    rows = first + jnp.arange(-6, ROWS + 6, dtype=jnp.int32)[:, None] + ROWS * jnp.arange(8, dtype=jnp.int32)[None, :]
    h = jnp.abs(jnp.sin(jnp.pi * (rows.astype(F32) + 0.5) / lat_total))
    g = jnp.where(rows % lat_total == 0, 0.0, jnp.abs(jnp.sin(jnp.pi * rows.astype(F32) / lat_total)))
    shape = (ROWS + 12, 8, 128)
    return (
        jnp.broadcast_to((1.0 / h)[:, :, None], shape),
        jnp.broadcast_to((g / 24.0)[:, :, None], shape),
    )


def local(sens, zonal, merid):
    lat_count, lon_count = lax.axis_size("lat"), lax.axis_size("lon")
    to_left, to_right, to_a, to_b = exchanges(lat_count, lon_count)
    hinv, gface = metric_tables(N * lat_count)
    left, right = make_columns_message(sens, zonal, merid)
    left = lax.ppermute(left, AXES, to_left)
    right = lax.ppermute(right, AXES, to_right)
    a, b = make_rows_message(sens, zonal, merid, left, right)
    a = lax.ppermute(a, AXES, to_a)
    b = lax.ppermute(b, AXES, to_b)
    return run_steps(sens, zonal, merid, left, right, a, b, hinv, gface)


def solution(mesh):
    placed = P(None, None, "lat", "lon")
    return jax.shard_map(local, mesh=mesh, in_specs=(placed,) * 3, out_specs=placed, check_vma=False)
```

```python
import jax
import jax.numpy as jnp
import numpy as np
from jax import lax
from jax.experimental import pallas as pl
from jax.experimental.pallas import tpu as pltpu
from jax.sharding import PartitionSpec as P

N = 360
LANES = 384
HALO = 6
ROWS = N // 8
FRONT = 8
MAIN_MIB = 40
PADDED = 384
UNROLL = 9
WIDE = -(-(ROWS + 6) // UNROLL) * UNROLL
F32 = jnp.float32
BF16 = jnp.bfloat16
AXES = ("lat", "lon")


def params(mebibytes):
    return pltpu.CompilerParams(vmem_limit_bytes=mebibytes * 2**20)


def lam_base(level, tracer):
    return 6 * (3 * level + tracer)


def z1_base(level):
    return 54 + 6 * level


def m1_base(level):
    return 72 + 3 * level


def z0_base(level):
    return 81 + 3 * level


def pack_columns(sw_ref, se_ref, zw_ref, ze_ref, mw_ref, me_ref, left_ref, right_ref):
    level = pl.program_id(1)
    odd = lax.axis_index("lon") % 2
    jobs = [(sw_ref, se_ref, t, HALO, lam_base(level, t)) for t in range(3)]
    jobs.append((zw_ref, ze_ref, 1, HALO, z1_base(level)))
    jobs.append((mw_ref, me_ref, 0, 3, m1_base(level)))
    jobs.append((zw_ref, ze_ref, 0, 3, z0_base(level)))
    rows = left_ref.shape[0]
    lane = lax.broadcasted_iota(jnp.int32, (rows, 128), 1)
    is_odd = (jnp.zeros((rows, 128), jnp.int32) + odd) == 1
    east = jnp.where(is_odd, right_ref[...], left_ref[...])
    west = jnp.where(is_odd, left_ref[...], right_ref[...])
    for w_ref, e_ref, k, width, base in jobs:
        both = jnp.where(lane < 64, w_ref[k, 0], e_ref[k, 0])
        turned_e = pltpu.roll(both, lax.rem(base + 30 - (HALO - width) + 128, 128), 1)
        turned_w = turned_e if width == HALO else pltpu.roll(both, base + 30, 1)
        east = jnp.where((lane >= base) & (lane < base + width), turned_e, east)
        west = jnp.where((lane >= base + 30) & (lane < base + 30 + width), turned_w, west)
    left_ref[...] = jnp.where(is_odd, west, east)
    right_ref[...] = jnp.where(is_odd, east, west)


def make_columns_message(sens, zonal, merid):
    part = N

    def spec(lead, step, tile):
        return pl.BlockSpec((lead, 1, part, 128), lambda r, l: (step, l, r, tile))

    whole = pl.BlockSpec((part, 128), lambda r, l: (r, 0))
    shape = jax.ShapeDtypeStruct((N, 128), F32)
    return pl.pallas_call(
        pack_columns,
        grid=(N // part, 3),
        in_specs=[spec(3, 0, 0), spec(3, 0, 2), spec(2, 0, 0), spec(2, 0, 2), spec(1, 1, 0), spec(1, 1, 2)],
        out_specs=[whole, whole],
        out_shape=[shape, shape],
        compiler_params=params(24),
        name="pack_columns",
    )(sens, sens, zonal, zonal, merid, merid)


def with_halo(own, east_msg, west_msg, base, width, lane):
    from_west = pltpu.roll(west_msg, (256 - width - base) % 128, 1)
    from_east = pltpu.roll(east_msg, (330 - base) % 128, 1)
    return jnp.where(lane < 104, own, jnp.where(lane < 116, from_east, from_west))


def sorted_by_side(left, right, odd, shape):
    is_odd = (jnp.zeros(shape, jnp.int32) + odd) == 1
    return jnp.where(is_odd, right, left), jnp.where(is_odd, left, right)


def flipped(rows, count):
    return jnp.concatenate([rows[count - 1 - k : count - k] for k in range(count)], axis=0)


def pack_rows(ss_ref, sn_ref, zs_ref, zn_ref, ms_ref, mn_ref, ls_ref, ln_ref, rs_ref, rn_ref, a_ref, b_ref):
    lat = lax.axis_index("lat")
    odd = lax.axis_index("lon") % 2
    lane = lax.broadcasted_iota(jnp.int32, (8, 128), 1)

    def mask(flag):
        return (jnp.zeros((8, 128), jnp.int32) + flag.astype(jnp.int32)) == 1

    turn_south, turn_north = mask(lat == 0), mask(lat == lax.axis_size("lat") - 1)
    lat_odd = mask(lat % 2)
    msgs_south = sorted_by_side(ls_ref[...], rs_ref[...], odd, (8, 128))
    msgs_north = sorted_by_side(ln_ref[...], rn_ref[...], odd, (8, 128))
    for level in range(3):
        slots = [(ss_ref, sn_ref, t, HALO, HALO, lam_base(level, t), 6 * t, 1.0) for t in range(3)]
        slots.append((ms_ref, mn_ref, 1, 6, 3, m1_base(level), 18, -1.0))
        slots.append((zs_ref, zn_ref, 1, 3, HALO, z1_base(level), 24, 1.0))
        slots.append((ms_ref, mn_ref, 0, 3, 0, 0, 27, -1.0))
        for s_ref, n_ref, k, count, width, base, at, sign in slots:
            for tile in range(3):
                cols = slice(tile * 128, (tile + 1) * 128)
                south, north = s_ref[k, level, :, cols], n_ref[k, level, :, cols]
                if tile == 2:
                    if width:
                        south = with_halo(south, *msgs_south, base, width, lane)
                        north = with_halo(north, *msgs_north, base, width, lane)
                    else:
                        south, north = jnp.where(lane < 104, south, 0.0), jnp.where(lane < 104, north, 0.0)
                south, north = south[:count], north[8 - count :]
                south = jnp.where(turn_south[:count], sign * flipped(south, count), south)
                north = jnp.where(turn_north[:count], sign * flipped(north, count), north)
                a_ref[level, pl.ds(at, count), cols] = jnp.where(lat_odd[:count], south, north)
                b_ref[level, pl.ds(at, count), cols] = jnp.where(lat_odd[:count], north, south)
        for out in (a_ref, b_ref):
            out[level, pl.ds(30, 2), :] = jnp.zeros((2, LANES), F32)


def make_rows_message(sens, zonal, merid, left, right):
    last = N // 8 - 1

    def spec(lead, block):
        return pl.BlockSpec((lead, 3, 8, LANES), lambda i: (0, 0, block, 0))

    def msg(block):
        return pl.BlockSpec((8, 128), lambda i: (block, 0))

    out = pl.BlockSpec((3, 32, LANES), lambda i: (0, 0, 0))
    shape = jax.ShapeDtypeStruct((3, 32, LANES), F32)
    return pl.pallas_call(
        pack_rows,
        grid=(1,),
        in_specs=[spec(3, 0), spec(3, last), spec(2, 0), spec(2, last), spec(2, 0), spec(2, last)]
        + [msg(0), msg(last), msg(0), msg(last)],
        out_specs=[out, out],
        out_shape=[shape, shape],
        compiler_params=params(24),
        name="pack_rows",
    )(sens, sens, zonal, zonal, merid, merid, left, left, right, right)


def permuted(values, table):
    high = values.astype(BF16)
    low = (values - high.astype(F32)).astype(BF16)
    return jnp.dot(jnp.concatenate([high, low], axis=1), table, preferred_element_type=F32)


def weights(total, scale):
    speed = jnp.abs(total) * 0.5
    lead = total * scale
    quad = lead * speed
    b = quad - quad * speed
    a = lead - quad - b
    c = (quad + b + b) * 12.0
    zero = jnp.zeros_like(b)
    return a, jnp.maximum(b, zero), jnp.minimum(b, zero), jnp.maximum(c, zero), jnp.minimum(c, zero)


def y_pass(load, wind, hinv, gface, store, first, last):
    scaled, faces, parts, eps, dee = {}, {}, {}, {}, {}

    def scaled_at(i):
        if i not in scaled:
            h = hinv(i)
            scaled[i] = [load(t, i) * h for t in range(3)]
        return scaled[i]

    def parts_at(f):
        if f not in parts:
            w = weights(wind(f - 1) + wind(f), gface(f))
            lo, hi = scaled_at(f - 1), scaled_at(f)
            phi = [hi[t] - lo[t] for t in range(3)]
            parts[f] = [[x * p for x in w] for p in phi]
        return parts[f]

    def eps_at(f):
        if f not in eps:
            p0, p1, pm = parts_at(f), parts_at(f + 1), parts_at(f - 1)
            eps[f] = [p0[t][0] - p1[t][1] - pm[t][2] for t in range(3)]
        return eps[f]

    def dee_at(i):
        if i not in dee:
            e0, e1 = eps_at(i), eps_at(i + 1)
            dee[i] = [e0[t] + e1[t] for t in range(3)]
        return dee[i]

    for i in range(first, last):
        dm, d0, dp = dee_at(i - 1), dee_at(i), dee_at(i + 1)
        p0, p1 = parts_at(i), parts_at(i + 1)
        for t in range(3):
            store(t, i, load(t, i) + (p0[t][4] + p1[t][3]) + (8.0 * d0[t] - (dm[t] + dp[t])))


def x_row(field, total, acc):
    w = [weights(total[p], 1.0 / 24.0) for p in range(3)]

    def one(f, base):
        phi = [f[0] - f[3], f[1] - f[0], f[2] - f[1]]
        a, bp, bm, cp, cm = [[w[p][k] * phi[p] for p in range(3)] for k in range(5)]
        e0 = a[0] - bp[1] - pltpu.roll(bm[2], 1, 1)
        e1 = a[1] - bp[2] - bm[0]
        e2 = a[2] - pltpu.roll(bp[0], 127, 1) - bm[1]
        s0, s1, s2 = 7.0 * e0, 7.0 * e1, 7.0 * e2
        out0 = (base[0] + cm[0]) + (cp[1] + s0) + (s1 - e2) - pltpu.roll(e2, 1, 1)
        out1 = (base[1] + cm[1]) + (cp[2] + s1) + (s2 - e0) - pltpu.roll(e0, 127, 1)
        out2 = (base[2] + cm[2]) + (s2 - e1) + pltpu.roll(cp[0] + (s0 - e1), 127, 1)
        return out0, out1, out2

    return [one(field[t], acc[t]) for t in range(3)]


def advance(
    s_ref, z_ref, m_ref, left_ref, right_ref, a_ref, b_ref, fwd_ref, inv_ref, metric_ref,
    out_ref, lam, zon, mer, acc, lam1, res, h_ref, g_ref,
):
    level = pl.program_id(0)
    lat_odd = lax.axis_index("lat") % 2
    lon_odd = lax.axis_index("lon") % 2
    chunk = N
    lane = lax.broadcasted_iota(jnp.int32, (chunk, 128), 1)

    @pl.when(level == 0)
    def _():
        both = metric_ref[lax.axis_index("lat")]
        for i in range(ROWS + 12):
            h_ref[i] = jnp.broadcast_to(both[0, :, i : i + 1], (8, 128))
            g_ref[i] = jnp.broadcast_to(both[1, :, i : i + 1], (8, 128))

    def take(r, _):
        rows = pl.ds(pl.multiple_of(r * chunk, 8), chunk)
        east_msg, west_msg = sorted_by_side(left_ref[rows, :], right_ref[rows, :], lon_odd, (chunk, 128))
        jobs = [(s_ref, t, HALO, lam_base(level, t), lam, t) for t in range(3)]
        jobs += [(z_ref, 1, HALO, z1_base(level), zon, 1), (z_ref, 0, 3, z0_base(level), zon, 0)]
        jobs += [(m_ref, 1, 3, m1_base(level), mer, 1), (m_ref, 0, 0, 0, mer, 0)]
        for ref, k, width, base, dst, j in jobs:
            tail = ref[k, 0, rows, 256:384]
            if width:
                tail = with_halo(tail, east_msg, west_msg, base, width, lane)
            else:
                tail = jnp.where(lane < 104, tail, 0.0)
            whole = jnp.concatenate([ref[k, 0, rows, 0:256], tail], axis=1)
            count = dst.shape[1]
            moved = permuted(whole, fwd_ref[:, : 128 * count])
            for p in range(count):
                dst[j, p, pl.ds(pl.multiple_of(FRONT + r * chunk, 8), chunk), :] = moved[:, p * 128 : (p + 1) * 128]
        return 0

    lax.fori_loop(0, N // chunk, take, 0)

    got_a, got_b = permuted(a_ref[0], fwd_ref[...]), permuted(b_ref[0], fwd_ref[...])
    odd = (jnp.zeros((32, LANES + 128), jnp.int32) + lat_odd) == 1
    north = jnp.where(odd, got_b, got_a)
    south = jnp.where(odd, got_a, got_b)
    slots = [(lam, t, 6, 6 * t) for t in range(3)]
    slots += [(mer, 1, 6, 18), (zon, 1, 3, 24), (mer, 0, 3, 27)]
    for dst, j, count, at in slots:
        for p in range(dst.shape[1]):
            cols = slice(p * 128, (p + 1) * 128)
            dst[j, p, pl.ds(FRONT - count, count), :] = south[at : at + count, cols]
            dst[j, p, pl.ds(FRONT + N, count), :] = north[at : at + count, cols]

    def strip(ref, j, p, i):
        return ref[j, p, pl.ds(FRONT + i, 8, stride=ROWS), :]

    def hinv(i):
        return h_ref[i + 6]

    def gface(f):
        return g_ref[f + 6]

    def y_one(p, _):
        def store(t, i, value):
            acc[t, p, i + 3] = value

        y_pass(lambda t, i: strip(lam, t, p, i), lambda i: strip(mer, 1, p, i), hinv, gface, store, -3, ROWS + 3)
        return 0

    lax.fori_loop(0, 3, y_one, 0)

    def zonal_total(step, i):
        z = [strip(zon, step, p, i) for p in range(4)]
        return [z[0] + z[3], z[1] + z[0], z[2] + z[1]]

    def x_one(q, _):
        for k in range(UNROLL):
            i = UNROLL * q + k
            field = [[strip(lam, t, p, i - 3) for p in range(4)] for t in range(3)]
            base = [[acc[t, p, i] for p in range(3)] for t in range(3)]
            new = x_row(field, zonal_total(1, i - 3), base)
            for t in range(3):
                for p in range(3):
                    lam1[t, p, i] = new[t][p]
        return 0

    lax.fori_loop(0, WIDE // UNROLL, x_one, 0)

    def y_two(p, _):
        def store(t, i, value):
            acc[t, p, i] = value

        y_pass(lambda t, i: lam1[t, p, i + 3], lambda i: strip(mer, 0, p, i), hinv, gface, store, 0, ROWS)
        for k in range(ROWS // 3):
            for t in range(3):
                lam1[t, 3, p * (ROWS // 3) + k + 3] = pltpu.roll(lam1[t, 2, p * (ROWS // 3) + k + 3], 1, 1)
        return 0

    lax.fori_loop(0, 3, y_two, 0)

    def x_two(q, _):
        for k in range(UNROLL):
            i = UNROLL * q + k
            field = [[lam1[t, p, i + 3] for p in range(4)] for t in range(3)]
            base = [[acc[t, p, i] for p in range(3)] for t in range(3)]
            new = x_row(field, zonal_total(0, i), base)
            for t in range(3):
                for p in range(3):
                    res[t, p, pl.ds(i, 8, stride=ROWS), :] = new[t][p]
        return 0

    lax.fori_loop(0, ROWS // UNROLL, x_two, 0)

    def give(r, _):
        rows = pl.ds(pl.multiple_of(r * chunk, 8), chunk)
        for t in range(3):
            phases = jnp.concatenate([res[t, p, rows, :] for p in range(3)], axis=1)
            out_ref[t, 0, rows, :] = permuted(phases, inv_ref[...])
        return 0

    lax.fori_loop(0, N // chunk, give, 0)


def run_steps(sens, zonal, merid, left, right, a, b):
    order = np.zeros((LANES, LANES + 128), np.float32)
    for at in range(LANES):
        order[3 * (at % 128) + at // 128, at] = 1.0
    for at in range(128):
        order[(3 * at - 1) % LANES, LANES + at] = 1.0
    fwd = jnp.asarray(np.concatenate([order, order]), BF16)
    back = order[:, :LANES].T
    inv = jnp.asarray(np.concatenate([back, back]), BF16)
    metric = metric_tables()

    def block(lead):
        return pl.BlockSpec((lead, 1, N, LANES), lambda l: (0, l, 0, 0))

    def whole(shape):
        return pl.BlockSpec(shape, lambda l: (0,) * len(shape))

    rows_msg = pl.BlockSpec((1, 32, LANES), lambda l: (l, 0, 0))
    return pl.pallas_call(
        advance,
        grid=(3,),
        in_specs=[block(3), block(2), block(2), whole((N, 128)), whole((N, 128)), rows_msg, rows_msg]
        + [whole(fwd.shape), whole(inv.shape), whole(metric.shape)],
        out_specs=block(3),
        out_shape=jax.ShapeDtypeStruct(sens.shape, F32),
        scratch_shapes=[
            pltpu.VMEM((3, 4, PADDED, 128), F32),
            pltpu.VMEM((2, 4, PADDED, 128), F32),
            pltpu.VMEM((2, 3, PADDED, 128), F32),
            pltpu.VMEM((3, 3, WIDE, 8, 128), F32),
            pltpu.VMEM((3, 4, WIDE, 8, 128), F32),
            pltpu.VMEM((3, 3, N, 128), F32),
            pltpu.VMEM((ROWS + 12, 8, 128), F32),
            pltpu.VMEM((ROWS + 12, 8, 128), F32),
        ],
        compiler_params=params(MAIN_MIB),
        name="advance",
    )(sens, zonal, merid, left, right, a, b, fwd, inv, metric)


def exchanges(lat_count, lon_count):
    def at(la, lo):
        return la * lon_count + lo % lon_count

    cells = [(la, lo) for la in range(lat_count) for lo in range(lon_count)]
    half = lon_count // 2
    left = [(at(la, lo), at(la, lo ^ 1)) for la, lo in cells]
    right = [(at(la, lo), at(la, lo + 1 if lo % 2 else lo - 1)) for la, lo in cells]
    a = [(at(la, lo), at(la ^ 1, lo)) for la, lo in cells]
    b = []
    for la, lo in cells:
        to = la + 1 if la % 2 else la - 1
        if to < 0 or to == lat_count:
            b.append((at(la, lo), at(la, lo + half)))
        else:
            b.append((at(la, lo), at(to, lo)))
    return left, right, a, b


def metric_tables():
    lat_count = lax.axis_size("lat")
    total = N * lat_count
    rows = N * np.arange(lat_count)[:, None, None] + ROWS * np.arange(8)[None, :, None] + np.arange(-6, ROWS + 6)
    h = np.abs(np.sin(np.pi * (rows + 0.5) / total))
    g = np.where(rows % total == 0, 0.0, np.abs(np.sin(np.pi * rows / total)))
    table = np.zeros((lat_count, 2, 8, 128), np.float32)
    table[:, 0, :, : ROWS + 12] = 1.0 / h
    table[:, 1, :, : ROWS + 12] = g / 24.0
    return jnp.asarray(table)


def local(sens, zonal, merid):
    lat_count, lon_count = lax.axis_size("lat"), lax.axis_size("lon")
    to_left, to_right, to_a, to_b = exchanges(lat_count, lon_count)
    left, right = make_columns_message(sens, zonal, merid)
    left = lax.ppermute(left, AXES, to_left)
    right = lax.ppermute(right, AXES, to_right)
    a, b = make_rows_message(sens, zonal, merid, left, right)
    a = lax.ppermute(a, AXES, to_a)
    b = lax.ppermute(b, AXES, to_b)
    return run_steps(sens, zonal, merid, left, right, a, b)


def solution(mesh):
    placed = P(None, None, "lat", "lon")
    return jax.shard_map(local, mesh=mesh, in_specs=(placed,) * 3, out_specs=placed, check_vma=False)
```

```python
import jax
import jax.numpy as jnp
import numpy as np
from jax import lax
from jax.experimental import pallas as pl
from jax.experimental.pallas import tpu as pltpu
from jax.sharding import PartitionSpec as P

N = 360
LANES = 384
HALO = 6
ROWS = N // 8
FRONT = 8
TAKE_MIB = 24
MAIN_MIB = 28
PADDED = 384
UNROLL = 9
F32 = jnp.float32
BF16 = jnp.bfloat16
AXES = ("lat", "lon")


def params(mebibytes):
    return pltpu.CompilerParams(vmem_limit_bytes=mebibytes * 2**20)


def lam_base(level, tracer):
    return 6 * (3 * level + tracer)


def z1_base(level):
    return 54 + 6 * level


def m1_base(level):
    return 72 + 3 * level


def z0_base(level):
    return 81 + 3 * level


def pack_columns(sw_ref, se_ref, zw_ref, ze_ref, mw_ref, me_ref, left_ref, right_ref):
    level = pl.program_id(1)
    odd = lax.axis_index("lon") % 2
    jobs = [(sw_ref, se_ref, t, HALO, lam_base(level, t)) for t in range(3)]
    jobs.append((zw_ref, ze_ref, 1, HALO, z1_base(level)))
    jobs.append((mw_ref, me_ref, 0, 3, m1_base(level)))
    jobs.append((zw_ref, ze_ref, 0, 3, z0_base(level)))
    rows = left_ref.shape[0]
    lane = lax.broadcasted_iota(jnp.int32, (rows, 128), 1)
    is_odd = (jnp.zeros((rows, 128), jnp.int32) + odd) == 1
    east = jnp.where(is_odd, right_ref[...], left_ref[...])
    west = jnp.where(is_odd, left_ref[...], right_ref[...])
    for w_ref, e_ref, k, width, base in jobs:
        both = jnp.where(lane < 64, w_ref[k, 0], e_ref[k, 0])
        turned_e = pltpu.roll(both, lax.rem(base + 30 - (HALO - width) + 128, 128), 1)
        turned_w = turned_e if width == HALO else pltpu.roll(both, base + 30, 1)
        east = jnp.where((lane >= base) & (lane < base + width), turned_e, east)
        west = jnp.where((lane >= base + 30) & (lane < base + 30 + width), turned_w, west)
    left_ref[...] = jnp.where(is_odd, west, east)
    right_ref[...] = jnp.where(is_odd, east, west)


def make_columns_message(sens, zonal, merid):
    part = N

    def spec(lead, step, tile):
        return pl.BlockSpec((lead, 1, part, 128), lambda r, l: (step, l, r, tile))

    whole = pl.BlockSpec((part, 128), lambda r, l: (r, 0))
    shape = jax.ShapeDtypeStruct((N, 128), F32)
    return pl.pallas_call(
        pack_columns,
        grid=(N // part, 3),
        in_specs=[spec(3, 0, 0), spec(3, 0, 2), spec(2, 0, 0), spec(2, 0, 2), spec(1, 1, 0), spec(1, 1, 2)],
        out_specs=[whole, whole],
        out_shape=[shape, shape],
        compiler_params=params(24),
        name="pack_columns",
    )(sens, sens, zonal, zonal, merid, merid)


def with_halo(own, east_msg, west_msg, base, width, lane):
    from_west = pltpu.roll(west_msg, (256 - width - base) % 128, 1)
    from_east = pltpu.roll(east_msg, (330 - base) % 128, 1)
    return jnp.where(lane < 104, own, jnp.where(lane < 116, from_east, from_west))


def sorted_by_side(left, right, odd, shape):
    is_odd = (jnp.zeros(shape, jnp.int32) + odd) == 1
    return jnp.where(is_odd, right, left), jnp.where(is_odd, left, right)


def flipped(rows, count):
    return jnp.concatenate([rows[count - 1 - k : count - k] for k in range(count)], axis=0)


def pack_rows(ss_ref, sn_ref, zs_ref, zn_ref, ms_ref, mn_ref, ls_ref, ln_ref, rs_ref, rn_ref, a_ref, b_ref):
    lat = lax.axis_index("lat")
    odd = lax.axis_index("lon") % 2
    lane = lax.broadcasted_iota(jnp.int32, (8, 128), 1)

    def mask(flag):
        return (jnp.zeros((8, 128), jnp.int32) + flag.astype(jnp.int32)) == 1

    turn_south, turn_north = mask(lat == 0), mask(lat == lax.axis_size("lat") - 1)
    lat_odd = mask(lat % 2)
    msgs_south = sorted_by_side(ls_ref[...], rs_ref[...], odd, (8, 128))
    msgs_north = sorted_by_side(ln_ref[...], rn_ref[...], odd, (8, 128))
    for level in range(3):
        slots = [(ss_ref, sn_ref, t, HALO, HALO, lam_base(level, t), 6 * t, 1.0) for t in range(3)]
        slots.append((ms_ref, mn_ref, 1, 6, 3, m1_base(level), 18, -1.0))
        slots.append((zs_ref, zn_ref, 1, 3, HALO, z1_base(level), 24, 1.0))
        slots.append((ms_ref, mn_ref, 0, 3, 0, 0, 27, -1.0))
        for s_ref, n_ref, k, count, width, base, at, sign in slots:
            for tile in range(3):
                cols = slice(tile * 128, (tile + 1) * 128)
                south, north = s_ref[k, level, :, cols], n_ref[k, level, :, cols]
                if tile == 2:
                    if width:
                        south = with_halo(south, *msgs_south, base, width, lane)
                        north = with_halo(north, *msgs_north, base, width, lane)
                    else:
                        south, north = jnp.where(lane < 104, south, 0.0), jnp.where(lane < 104, north, 0.0)
                south, north = south[:count], north[8 - count :]
                south = jnp.where(turn_south[:count], sign * flipped(south, count), south)
                north = jnp.where(turn_north[:count], sign * flipped(north, count), north)
                a_ref[level, pl.ds(at, count), cols] = jnp.where(lat_odd[:count], south, north)
                b_ref[level, pl.ds(at, count), cols] = jnp.where(lat_odd[:count], north, south)
        for out in (a_ref, b_ref):
            out[level, pl.ds(30, 2), :] = jnp.zeros((2, LANES), F32)


def make_rows_message(rims, left, right):
    last = N // 8 - 1

    def spec(lead):
        return pl.BlockSpec((lead, 3, 8, LANES), lambda i: (0, 0, 0, 0))

    def msg(block):
        return pl.BlockSpec((8, 128), lambda i: (block, 0))

    out = pl.BlockSpec((3, 32, LANES), lambda i: (0, 0, 0))
    shape = jax.ShapeDtypeStruct((3, 32, LANES), F32)
    return pl.pallas_call(
        pack_rows,
        grid=(1,),
        in_specs=[spec(3), spec(3), spec(2), spec(2), spec(2), spec(2), msg(0), msg(last), msg(0), msg(last)],
        out_specs=[out, out],
        out_shape=[shape, shape],
        compiler_params=params(24),
        name="pack_rows",
    )(*(rim for pair in rims for rim in pair), left, left, right, right)


def permuted(values, table):
    high = values.astype(BF16)
    low = (values - high.astype(F32)).astype(BF16)
    return jnp.dot(jnp.concatenate([high, low], axis=1), table, preferred_element_type=F32)


def weights(total, scale):
    speed = jnp.abs(total) * 0.5
    lead = total * scale
    quad = lead * speed
    b = quad - quad * speed
    a = lead - quad - b
    c = (quad + b + b) * 12.0
    zero = jnp.zeros_like(b)
    return a, jnp.maximum(b, zero), jnp.minimum(b, zero), jnp.maximum(c, zero), jnp.minimum(c, zero)


def y_pass(load, wind, hinv, gface, store, first, last):
    scaled, faces, parts, eps, dee = {}, {}, {}, {}, {}

    def scaled_at(i):
        if i not in scaled:
            h = hinv(i)
            scaled[i] = [load(t, i) * h for t in range(3)]
        return scaled[i]

    def parts_at(f):
        if f not in parts:
            w = weights(wind(f - 1) + wind(f), gface(f))
            lo, hi = scaled_at(f - 1), scaled_at(f)
            phi = [hi[t] - lo[t] for t in range(3)]
            parts[f] = [[x * p for x in w] for p in phi]
        return parts[f]

    def eps_at(f):
        if f not in eps:
            p0, p1, pm = parts_at(f), parts_at(f + 1), parts_at(f - 1)
            eps[f] = [p0[t][0] - p1[t][1] - pm[t][2] for t in range(3)]
        return eps[f]

    def dee_at(i):
        if i not in dee:
            e0, e1 = eps_at(i), eps_at(i + 1)
            dee[i] = [e0[t] + e1[t] for t in range(3)]
        return dee[i]

    for i in range(first, last):
        dm, d0, dp = dee_at(i - 1), dee_at(i), dee_at(i + 1)
        p0, p1 = parts_at(i), parts_at(i + 1)
        for t in range(3):
            store(t, i, load(t, i) + (p0[t][4] + p1[t][3]) + (8.0 * d0[t] - (dm[t] + dp[t])))


def x_row(field, total, acc):
    w = [weights(total[p], 1.0 / 24.0) for p in range(3)]

    def one(f, base):
        phi = [f[0] - f[3], f[1] - f[0], f[2] - f[1]]
        a, bp, bm, cp, cm = [[w[p][k] * phi[p] for p in range(3)] for k in range(5)]
        e0 = a[0] - bp[1] - pltpu.roll(bm[2], 1, 1)
        e1 = a[1] - bp[2] - bm[0]
        e2 = a[2] - pltpu.roll(bp[0], 127, 1) - bm[1]
        s0, s1, s2 = 7.0 * e0, 7.0 * e1, 7.0 * e2
        out0 = (base[0] + cm[0]) + (cp[1] + s0) + (s1 - e2) - pltpu.roll(e2, 1, 1)
        out1 = (base[1] + cm[1]) + (cp[2] + s1) + (s2 - e0) - pltpu.roll(e0, 127, 1)
        out2 = (base[2] + cm[2]) + (s2 - e1) + pltpu.roll(cp[0] + (s0 - e1), 127, 1)
        return out0, out1, out2

    return [one(field[t], acc[t]) for t in range(3)]


def take(s_ref, z_ref, m_ref, left_ref, right_ref, fwd_ref, lam_ref, zon_ref, mer_ref):
    level = pl.program_id(0)
    lane = lax.broadcasted_iota(jnp.int32, (N, 128), 1)
    lon_odd = lax.axis_index("lon") % 2
    east_msg, west_msg = sorted_by_side(left_ref[...], right_ref[...], lon_odd, (N, 128))
    jobs = [(s_ref, t, HALO, lam_base(level, t), lam_ref, t) for t in range(3)]
    jobs += [(z_ref, 1, HALO, z1_base(level), zon_ref, 1), (z_ref, 0, 3, z0_base(level), zon_ref, 0)]
    jobs += [(m_ref, 1, 3, m1_base(level), mer_ref, 1), (m_ref, 0, 0, 0, mer_ref, 0)]
    for ref, k, width, base, dst, j in jobs:
        tail = ref[k, 0, :, 256:384]
        if width:
            tail = with_halo(tail, east_msg, west_msg, base, width, lane)
        else:
            tail = jnp.where(lane < 104, tail, 0.0)
        whole = jnp.concatenate([ref[k, 0, :, 0:256], tail], axis=1)
        count = dst.shape[2]
        moved = permuted(whole, fwd_ref[:, : 128 * count])
        for p in range(count):
            dst[level, j, p, pl.ds(FRONT, N), :] = moved[:, p * 128 : (p + 1) * 128]


def advance(
    lam, zon, mer, a_ref, b_ref, fwd_ref, inv_ref, metric_ref,
    out_ref, lam_e, zon_e, mer_e, acc, lam1, res, h_ref, g_ref,
):
    level = pl.program_id(0)
    lat_odd = lax.axis_index("lat") % 2
    sublane = lax.broadcasted_iota(jnp.int32, (8, 128), 0)

    @pl.when(level == 0)
    def _():
        both = metric_ref[lax.axis_index("lat")]
        for i in range(ROWS + 12):
            h_ref[i] = jnp.broadcast_to(both[0, :, i : i + 1], (8, 128))
            g_ref[i] = jnp.broadcast_to(both[1, :, i : i + 1], (8, 128))

    def strip(ref, j, p, i):
        return ref[level, j, p, pl.ds(FRONT + i, 8, stride=ROWS), :]

    got_a, got_b = permuted(a_ref[0], fwd_ref[...]), permuted(b_ref[0], fwd_ref[...])
    odd = (jnp.zeros((32, LANES + 128), jnp.int32) + lat_odd) == 1
    north = jnp.where(odd, got_b, got_a)
    south = jnp.where(odd, got_a, got_b)
    slots = [(lam, lam_e, t, 6, 6 * t) for t in range(3)]
    slots += [(mer, mer_e, 1, 6, 18), (zon, zon_e, 1, 3, 24), (mer, mer_e, 0, 3, 27)]
    for src, dst, j, count, at in slots:
        for p in range(dst.shape[1]):
            cols = slice(p * 128, (p + 1) * 128)
            for k in range(count):
                low = jnp.broadcast_to(south[at + k : at + k + 1, cols], (8, 128))
                dst[j, p, HALO - count + k] = jnp.where(sublane == 0, low, strip(src, j, p, k - count))
                high = jnp.broadcast_to(north[at + k : at + k + 1, cols], (8, 128))
                dst[j, p, HALO + k] = jnp.where(sublane == 7, high, strip(src, j, p, ROWS + k))

    def row(ref, edge, j, p, i):
        if i < 0:
            return edge[j, p, i + HALO]
        if i >= ROWS:
            return edge[j, p, i - ROWS + HALO]
        return strip(ref, j, p, i)

    def hinv(i):
        return h_ref[i + 6]

    def gface(f):
        return g_ref[f + 6]

    def y_one(p, _):
        def store(t, i, value):
            acc[t, p, i + 3] = value

        y_pass(
            lambda t, i: row(lam, lam_e, t, p, i), lambda i: row(mer, mer_e, 1, p, i),
            hinv, gface, store, -3, ROWS + 3,
        )
        return 0

    lax.fori_loop(0, 3, y_one, 0)

    def x_first(i, fetch):
        field = [[fetch(lam, lam_e, t, p, i) for p in range(4)] for t in range(3)]
        z = [fetch(zon, zon_e, 1, p, i) for p in range(4)]
        base = [[acc[t, p, i + 3] for p in range(3)] for t in range(3)]
        new = x_row(field, [z[0] + z[3], z[1] + z[0], z[2] + z[1]], base)
        for t in range(3):
            for p in range(3):
                lam1[t, p, i + 3] = new[t][p]

    for i in (-3, -2, -1, ROWS, ROWS + 1, ROWS + 2):
        x_first(i, row)

    def x_one(q, _):
        for k in range(UNROLL):
            x_first(UNROLL * q + k, lambda ref, edge, j, p, i: strip(ref, j, p, i))
        return 0

    lax.fori_loop(0, ROWS // UNROLL, x_one, 0)

    def y_two(p, _):
        def store(t, i, value):
            acc[t, p, i] = value

        y_pass(
            lambda t, i: lam1[t, p, i + 3], lambda i: row(mer, mer_e, 0, p, i),
            hinv, gface, store, 0, ROWS,
        )
        for k in range(ROWS // 3):
            for t in range(3):
                lam1[t, 3, p * (ROWS // 3) + k + 3] = pltpu.roll(lam1[t, 2, p * (ROWS // 3) + k + 3], 1, 1)
        return 0

    lax.fori_loop(0, 3, y_two, 0)

    def x_two(q, _):
        for k in range(UNROLL):
            i = UNROLL * q + k
            field = [[lam1[t, p, i + 3] for p in range(4)] for t in range(3)]
            z = [strip(zon, 0, p, i) for p in range(4)]
            base = [[acc[t, p, i] for p in range(3)] for t in range(3)]
            new = x_row(field, [z[0] + z[3], z[1] + z[0], z[2] + z[1]], base)
            for t in range(3):
                for p in range(3):
                    res[t, p, pl.ds(i, 8, stride=ROWS), :] = new[t][p]
        return 0

    lax.fori_loop(0, ROWS // UNROLL, x_two, 0)

    for t in range(3):
        phases = jnp.concatenate([res[t, p] for p in range(3)], axis=1)
        out_ref[t, 0] = permuted(phases, inv_ref[...])


def column_tables():
    order = np.zeros((LANES, LANES + 128), np.float32)
    for at in range(LANES):
        order[3 * (at % 128) + at // 128, at] = 1.0
    for at in range(128):
        order[(3 * at - 1) % LANES, LANES + at] = 1.0
    fwd = jnp.asarray(np.concatenate([order, order]), BF16)
    back = order[:, :LANES].T
    inv = jnp.asarray(np.concatenate([back, back]), BF16)
    return fwd, inv


def block(lead):
    return pl.BlockSpec((lead, 1, N, LANES), lambda l: (0, l, 0, 0))


def whole(shape):
    return pl.BlockSpec(shape, lambda l: (0,) * len(shape))


def phased(*lead):
    shape = lead + (PADDED, 128)
    return pl.BlockSpec(memory_space=pltpu.VMEM), pltpu.VMEM((3,) + shape, F32)


PHASED = [phased(3, 4), phased(2, 4), phased(2, 3)]


def take_columns(sens, zonal, merid, left, right, fwd):
    return pl.pallas_call(
        take,
        grid=(3,),
        in_specs=[block(3), block(2), block(2), whole((N, 128)), whole((N, 128)), whole(fwd.shape)],
        out_specs=[spec for spec, _ in PHASED],
        out_shape=[shape for _, shape in PHASED],
        compiler_params=params(TAKE_MIB),
        cost_estimate=pl.CostEstimate(flops=9 * 10**9, bytes_accessed=26 * 10**6, transcendentals=0),
        name="take",
    )(sens, zonal, merid, left, right, fwd)


def run_steps(lam, zon, mer, a, b, fwd, inv):
    metric = metric_tables()
    rows_msg = pl.BlockSpec((1, 32, LANES), lambda l: (l, 0, 0))
    return pl.pallas_call(
        advance,
        grid=(3,),
        in_specs=[spec for spec, _ in PHASED] + [rows_msg, rows_msg]
        + [whole(fwd.shape), whole(inv.shape), whole(metric.shape)],
        out_specs=block(3),
        out_shape=jax.ShapeDtypeStruct((3, 3, N, N), F32),
        scratch_shapes=[
            pltpu.VMEM((3, 4, 2 * HALO, 8, 128), F32),
            pltpu.VMEM((2, 4, 2 * HALO, 8, 128), F32),
            pltpu.VMEM((2, 3, 2 * HALO, 8, 128), F32),
            pltpu.VMEM((3, 3, ROWS + 6, 8, 128), F32),
            pltpu.VMEM((3, 4, ROWS + 6, 8, 128), F32),
            pltpu.VMEM((3, 3, N, 128), F32),
            pltpu.VMEM((ROWS + 12, 8, 128), F32),
            pltpu.VMEM((ROWS + 12, 8, 128), F32),
        ],
        compiler_params=params(MAIN_MIB),
        name="advance",
    )(lam, zon, mer, a, b, fwd, inv, metric)


def exchanges(lat_count, lon_count):
    def at(la, lo):
        return la * lon_count + lo % lon_count

    cells = [(la, lo) for la in range(lat_count) for lo in range(lon_count)]
    half = lon_count // 2
    left = [(at(la, lo), at(la, lo ^ 1)) for la, lo in cells]
    right = [(at(la, lo), at(la, lo + 1 if lo % 2 else lo - 1)) for la, lo in cells]
    a = [(at(la, lo), at(la ^ 1, lo)) for la, lo in cells]
    b = []
    for la, lo in cells:
        to = la + 1 if la % 2 else la - 1
        if to < 0 or to == lat_count:
            b.append((at(la, lo), at(la, lo + half)))
        else:
            b.append((at(la, lo), at(to, lo)))
    return left, right, a, b


def metric_tables():
    lat_count = lax.axis_size("lat")
    total = N * lat_count
    rows = N * np.arange(lat_count)[:, None, None] + ROWS * np.arange(8)[None, :, None] + np.arange(-6, ROWS + 6)
    h = np.abs(np.sin(np.pi * (rows + 0.5) / total))
    g = np.where(rows % total == 0, 0.0, np.abs(np.sin(np.pi * rows / total)))
    table = np.zeros((lat_count, 2, 8, 128), np.float32)
    table[:, 0, :, : ROWS + 12] = 1.0 / h
    table[:, 1, :, : ROWS + 12] = g / 24.0
    return jnp.asarray(table)


def local(sens, zonal, merid):
    lat_count, lon_count = lax.axis_size("lat"), lax.axis_size("lon")
    to_left, to_right, to_a, to_b = exchanges(lat_count, lon_count)
    rims = [(x[:, :, :8], x[:, :, N - 8 :]) for x in (sens, zonal, merid)]
    sens, zonal, merid = [pltpu.with_memory_space_constraint(x, pltpu.HBM) for x in (sens, zonal, merid)]
    left, right = make_columns_message(sens, zonal, merid)
    left = lax.ppermute(left, AXES, to_left)
    right = lax.ppermute(right, AXES, to_right)
    a, b = make_rows_message(rims, left, right)
    fwd, inv = column_tables()
    lam, zon, mer = take_columns(sens, zonal, merid, left, right, fwd)
    a = lax.ppermute(a, AXES, to_a)
    b = lax.ppermute(b, AXES, to_b)
    return run_steps(lam, zon, mer, a, b, fwd, inv)


def solution(mesh):
    placed = P(None, None, "lat", "lon")
    return jax.shard_map(local, mesh=mesh, in_specs=(placed,) * 3, out_specs=placed, check_vma=False)
```

```python
import jax
import jax.numpy as jnp
import numpy as np
from jax import lax
from jax.experimental import pallas as pl
from jax.experimental.pallas import tpu as pltpu
from jax.sharding import PartitionSpec as P

N = 360
LANES = 384
HALO = 6
ROWS = N // 8
FRONT = 8
TAKE_MIB = 24
MAIN_MIB = 28
PADDED = 384
UNROLL = 9
F32 = jnp.float32
BF16 = jnp.bfloat16
AXES = ("lat", "lon")


def params(mebibytes):
    return pltpu.CompilerParams(vmem_limit_bytes=mebibytes * 2**20)


def lam_base(level, tracer):
    return 6 * (3 * level + tracer)


def z1_base(level):
    return 54 + 6 * level


def m1_base(level):
    return 72 + 3 * level


def z0_base(level):
    return 81 + 3 * level


def pack_columns(sw_ref, se_ref, zw_ref, ze_ref, mw_ref, me_ref, left_ref, right_ref):
    level = pl.program_id(1)
    odd = lax.axis_index("lon") % 2
    jobs = [(sw_ref, se_ref, t, HALO, lam_base(level, t)) for t in range(3)]
    jobs.append((zw_ref, ze_ref, 1, HALO, z1_base(level)))
    jobs.append((mw_ref, me_ref, 0, 3, m1_base(level)))
    jobs.append((zw_ref, ze_ref, 0, 3, z0_base(level)))
    rows = left_ref.shape[0]
    lane = lax.broadcasted_iota(jnp.int32, (rows, 128), 1)
    is_odd = (jnp.zeros((rows, 128), jnp.int32) + odd) == 1
    east = jnp.where(is_odd, right_ref[...], left_ref[...])
    west = jnp.where(is_odd, left_ref[...], right_ref[...])
    for w_ref, e_ref, k, width, base in jobs:
        both = jnp.where(lane < 64, w_ref[k, 0], e_ref[k, 0])
        turned_e = pltpu.roll(both, lax.rem(base + 30 - (HALO - width) + 128, 128), 1)
        turned_w = turned_e if width == HALO else pltpu.roll(both, base + 30, 1)
        east = jnp.where((lane >= base) & (lane < base + width), turned_e, east)
        west = jnp.where((lane >= base + 30) & (lane < base + 30 + width), turned_w, west)
    left_ref[...] = jnp.where(is_odd, west, east)
    right_ref[...] = jnp.where(is_odd, east, west)


def make_columns_message(sens, zonal, merid):
    part = N

    def spec(lead, step, tile):
        return pl.BlockSpec((lead, 1, part, 128), lambda r, l: (step, l, r, tile))

    whole = pl.BlockSpec((part, 128), lambda r, l: (r, 0))
    shape = jax.ShapeDtypeStruct((N, 128), F32)
    return pl.pallas_call(
        pack_columns,
        grid=(N // part, 3),
        in_specs=[spec(3, 0, 0), spec(3, 0, 2), spec(2, 0, 0), spec(2, 0, 2), spec(1, 1, 0), spec(1, 1, 2)],
        out_specs=[whole, whole],
        out_shape=[shape, shape],
        compiler_params=params(24),
        name="pack_columns",
    )(sens, sens, zonal, zonal, merid, merid)


def with_halo(own, east_msg, west_msg, base, width, lane):
    from_west = pltpu.roll(west_msg, (256 - width - base) % 128, 1)
    from_east = pltpu.roll(east_msg, (330 - base) % 128, 1)
    return jnp.where(lane < 104, own, jnp.where(lane < 116, from_east, from_west))


def sorted_by_side(left, right, odd, shape):
    is_odd = (jnp.zeros(shape, jnp.int32) + odd) == 1
    return jnp.where(is_odd, right, left), jnp.where(is_odd, left, right)


def flipped(rows, count):
    return jnp.concatenate([rows[count - 1 - k : count - k] for k in range(count)], axis=0)


def pack_rows(ss_ref, sn_ref, zs_ref, zn_ref, ms_ref, mn_ref, ls_ref, ln_ref, rs_ref, rn_ref, a_ref, b_ref):
    lat = lax.axis_index("lat")
    odd = lax.axis_index("lon") % 2
    lane = lax.broadcasted_iota(jnp.int32, (8, 128), 1)

    def mask(flag):
        return (jnp.zeros((8, 128), jnp.int32) + flag.astype(jnp.int32)) == 1

    turn_south, turn_north = mask(lat == 0), mask(lat == lax.axis_size("lat") - 1)
    lat_odd = mask(lat % 2)
    msgs_south = sorted_by_side(ls_ref[...], rs_ref[...], odd, (8, 128))
    msgs_north = sorted_by_side(ln_ref[...], rn_ref[...], odd, (8, 128))
    for level in range(3):
        slots = [(ss_ref, sn_ref, t, HALO, HALO, lam_base(level, t), 6 * t, 1.0) for t in range(3)]
        slots.append((ms_ref, mn_ref, 1, 6, 3, m1_base(level), 18, -1.0))
        slots.append((zs_ref, zn_ref, 1, 3, HALO, z1_base(level), 24, 1.0))
        slots.append((ms_ref, mn_ref, 0, 3, 0, 0, 27, -1.0))
        for s_ref, n_ref, k, count, width, base, at, sign in slots:
            for tile in range(3):
                cols = slice(tile * 128, (tile + 1) * 128)
                south, north = s_ref[k, level, :, cols], n_ref[k, level, :, cols]
                if tile == 2:
                    if width:
                        south = with_halo(south, *msgs_south, base, width, lane)
                        north = with_halo(north, *msgs_north, base, width, lane)
                    else:
                        south, north = jnp.where(lane < 104, south, 0.0), jnp.where(lane < 104, north, 0.0)
                south, north = south[:count], north[8 - count :]
                south = jnp.where(turn_south[:count], sign * flipped(south, count), south)
                north = jnp.where(turn_north[:count], sign * flipped(north, count), north)
                a_ref[level, pl.ds(at, count), cols] = jnp.where(lat_odd[:count], south, north)
                b_ref[level, pl.ds(at, count), cols] = jnp.where(lat_odd[:count], north, south)
        for out in (a_ref, b_ref):
            out[level, pl.ds(30, 2), :] = jnp.zeros((2, LANES), F32)


def make_rows_message(rims, left, right):
    last = N // 8 - 1

    def spec(lead):
        return pl.BlockSpec((lead, 3, 8, LANES), lambda i: (0, 0, 0, 0))

    def msg(block):
        return pl.BlockSpec((8, 128), lambda i: (block, 0))

    out = pl.BlockSpec((3, 32, LANES), lambda i: (0, 0, 0))
    shape = jax.ShapeDtypeStruct((3, 32, LANES), F32)
    return pl.pallas_call(
        pack_rows,
        grid=(1,),
        in_specs=[spec(3), spec(3), spec(2), spec(2), spec(2), spec(2), msg(0), msg(last), msg(0), msg(last)],
        out_specs=[out, out],
        out_shape=[shape, shape],
        compiler_params=params(24),
        name="pack_rows",
    )(*(rim for pair in rims for rim in pair), left, left, right, right)


def permuted(values, table):
    high = values.astype(BF16)
    low = (values - high.astype(F32)).astype(BF16)
    return jnp.dot(jnp.concatenate([high, low], axis=1), table, preferred_element_type=F32)


def weights(total, scale):
    speed = jnp.abs(total) * 0.5
    lead = total * scale
    quad = lead * speed
    b = quad - quad * speed
    a = lead - quad - b
    c = (quad + b + b) * 12.0
    zero = jnp.zeros_like(b)
    return a, jnp.maximum(b, zero), jnp.minimum(b, zero), jnp.maximum(c, zero), jnp.minimum(c, zero)


def y_pass(load, wind, hinv, gface, store, first, last):
    scaled, faces, parts, eps, dee = {}, {}, {}, {}, {}

    def scaled_at(i):
        if i not in scaled:
            h = hinv(i)
            scaled[i] = [load(t, i) * h for t in range(3)]
        return scaled[i]

    def parts_at(f):
        if f not in parts:
            w = weights(wind(f - 1) + wind(f), gface(f))
            lo, hi = scaled_at(f - 1), scaled_at(f)
            phi = [hi[t] - lo[t] for t in range(3)]
            parts[f] = [[x * p for x in w] for p in phi]
        return parts[f]

    def eps_at(f):
        if f not in eps:
            p0, p1, pm = parts_at(f), parts_at(f + 1), parts_at(f - 1)
            eps[f] = [p0[t][0] - p1[t][1] - pm[t][2] for t in range(3)]
        return eps[f]

    def dee_at(i):
        if i not in dee:
            e0, e1 = eps_at(i), eps_at(i + 1)
            dee[i] = [e0[t] + e1[t] for t in range(3)]
        return dee[i]

    for i in range(first, last):
        dm, d0, dp = dee_at(i - 1), dee_at(i), dee_at(i + 1)
        p0, p1 = parts_at(i), parts_at(i + 1)
        for t in range(3):
            store(t, i, load(t, i) + (p0[t][4] + p1[t][3]) + (8.0 * d0[t] - (dm[t] + dp[t])))


def x_row(field, total, acc):
    w = [weights(total[p], 1.0 / 24.0) for p in range(3)]

    def one(f, base):
        phi = [f[0] - f[3], f[1] - f[0], f[2] - f[1]]
        a, bp, bm, cp, cm = [[w[p][k] * phi[p] for p in range(3)] for k in range(5)]
        e0 = a[0] - bp[1] - pltpu.roll(bm[2], 1, 1)
        e1 = a[1] - bp[2] - bm[0]
        e2 = a[2] - pltpu.roll(bp[0], 127, 1) - bm[1]
        s0, s1, s2 = 7.0 * e0, 7.0 * e1, 7.0 * e2
        out0 = (base[0] + cm[0]) + (cp[1] + s0) + (s1 - e2) - pltpu.roll(e2, 1, 1)
        out1 = (base[1] + cm[1]) + (cp[2] + s1) + (s2 - e0) - pltpu.roll(e0, 127, 1)
        out2 = (base[2] + cm[2]) + (s2 - e1) + pltpu.roll(cp[0] + (s0 - e1), 127, 1)
        return out0, out1, out2

    return [one(field[t], acc[t]) for t in range(3)]


def take(s_ref, z_ref, m_ref, left_ref, right_ref, fwd_ref, lam_ref, zon_ref, mer_ref):
    level = pl.program_id(0)
    lane = lax.broadcasted_iota(jnp.int32, (N, 128), 1)
    lon_odd = lax.axis_index("lon") % 2
    east_msg, west_msg = sorted_by_side(left_ref[...], right_ref[...], lon_odd, (N, 128))
    jobs = [(s_ref, lam_ref, [(t, HALO, lam_base(level, t)) for t in range(3)])]
    jobs.append((z_ref, zon_ref, [(1, HALO, z1_base(level)), (0, 3, z0_base(level))]))
    jobs.append((m_ref, mer_ref, [(0, 3, m1_base(level))]))
    for ref, dst, fields in jobs:
        stack = []
        for k, width, base in fields:
            tail = ref[k, 0, :, 256:384]
            tail = with_halo(tail, east_msg, west_msg, base, width, lane)
            stack.append(jnp.concatenate([ref[k, 0, :, 0:256], tail], axis=1))
        count = dst.shape[2]
        moved = permuted(jnp.concatenate(stack, axis=0), fwd_ref[:, : 128 * count])
        for n, (k, _, _) in enumerate(fields):
            for p in range(count):
                dst[level, k, p, pl.ds(FRONT, N), :] = moved[n * N : (n + 1) * N, p * 128 : (p + 1) * 128]


def take_alone(m_ref, fwd_ref, mer_ref):
    lane = lax.broadcasted_iota(jnp.int32, (N, 128), 1)
    tail = jnp.where(lane < 104, m_ref[0, 0, :, 256:384], 0.0)
    own = jnp.concatenate([m_ref[0, 0, :, 0:256], tail], axis=1)
    moved = permuted(own, fwd_ref[:, :LANES])
    for p in range(3):
        mer_ref[pl.program_id(0), 0, p, pl.ds(FRONT, N), :] = moved[:, p * 128 : (p + 1) * 128]


def advance(
    lam, zon, mer, mer_now, a_ref, b_ref, fwd_ref, inv_ref, metric_ref,
    out_ref, lam_e, zon_e, mer_e, acc, lam1, res, h_ref, g_ref,
):
    level = pl.program_id(0)
    lat_odd = lax.axis_index("lat") % 2
    sublane = lax.broadcasted_iota(jnp.int32, (8, 128), 0)

    @pl.when(level == 0)
    def _():
        both = metric_ref[lax.axis_index("lat")]
        for i in range(ROWS + 12):
            h_ref[i] = jnp.broadcast_to(both[0, :, i : i + 1], (8, 128))
            g_ref[i] = jnp.broadcast_to(both[1, :, i : i + 1], (8, 128))

    def strip(ref, j, p, i):
        return ref[level, j, p, pl.ds(FRONT + i, 8, stride=ROWS), :]

    got_a, got_b = permuted(a_ref[0], fwd_ref[...]), permuted(b_ref[0], fwd_ref[...])
    odd = (jnp.zeros((32, LANES + 128), jnp.int32) + lat_odd) == 1
    north = jnp.where(odd, got_b, got_a)
    south = jnp.where(odd, got_a, got_b)
    slots = [(lam, t, lam_e, t, 6, 6 * t) for t in range(3)]
    slots += [(mer, 0, mer_e, 1, 6, 18), (zon, 1, zon_e, 1, 3, 24), (mer_now, 0, mer_e, 0, 3, 27)]
    for src, k_src, dst, j, count, at in slots:
        for p in range(dst.shape[1]):
            cols = slice(p * 128, (p + 1) * 128)
            for k in range(count):
                low = jnp.broadcast_to(south[at + k : at + k + 1, cols], (8, 128))
                dst[j, p, HALO - count + k] = jnp.where(sublane == 0, low, strip(src, k_src, p, k - count))
                high = jnp.broadcast_to(north[at + k : at + k + 1, cols], (8, 128))
                dst[j, p, HALO + k] = jnp.where(sublane == 7, high, strip(src, k_src, p, ROWS + k))

    def row(ref, edge, j, p, i, k=None):
        if i < 0:
            return edge[j, p, i + HALO]
        if i >= ROWS:
            return edge[j, p, i - ROWS + HALO]
        return strip(ref, j if k is None else k, p, i)

    def hinv(i):
        return h_ref[i + 6]

    def gface(f):
        return g_ref[f + 6]

    def y_one(p, _):
        def store(t, i, value):
            acc[t, p, i + 3] = value

        y_pass(
            lambda t, i: row(lam, lam_e, t, p, i), lambda i: row(mer, mer_e, 1, p, i, 0),
            hinv, gface, store, -3, ROWS + 3,
        )
        return 0

    lax.fori_loop(0, 3, y_one, 0)

    def x_first(i, fetch):
        field = [[fetch(lam, lam_e, t, p, i) for p in range(4)] for t in range(3)]
        z = [fetch(zon, zon_e, 1, p, i) for p in range(4)]
        base = [[acc[t, p, i + 3] for p in range(3)] for t in range(3)]
        new = x_row(field, [z[0] + z[3], z[1] + z[0], z[2] + z[1]], base)
        for t in range(3):
            for p in range(3):
                lam1[t, p, i + 3] = new[t][p]

    for i in (-3, -2, -1, ROWS, ROWS + 1, ROWS + 2):
        x_first(i, row)

    def x_one(q, _):
        for k in range(UNROLL):
            x_first(UNROLL * q + k, lambda ref, edge, j, p, i: strip(ref, j, p, i))
        return 0

    lax.fori_loop(0, ROWS // UNROLL, x_one, 0)

    def y_two(p, _):
        def store(t, i, value):
            acc[t, p, i] = value

        y_pass(
            lambda t, i: lam1[t, p, i + 3], lambda i: row(mer_now, mer_e, 0, p, i),
            hinv, gface, store, 0, ROWS,
        )
        for k in range(ROWS // 3):
            for t in range(3):
                lam1[t, 3, p * (ROWS // 3) + k + 3] = pltpu.roll(lam1[t, 2, p * (ROWS // 3) + k + 3], 1, 1)
        return 0

    lax.fori_loop(0, 3, y_two, 0)

    def x_two(q, _):
        for k in range(UNROLL):
            i = UNROLL * q + k
            field = [[lam1[t, p, i + 3] for p in range(4)] for t in range(3)]
            z = [strip(zon, 0, p, i) for p in range(4)]
            base = [[acc[t, p, i] for p in range(3)] for t in range(3)]
            new = x_row(field, [z[0] + z[3], z[1] + z[0], z[2] + z[1]], base)
            for t in range(3):
                for p in range(3):
                    res[t, p, pl.ds(i, 8, stride=ROWS), :] = new[t][p]
        return 0

    lax.fori_loop(0, ROWS // UNROLL, x_two, 0)

    phases = jnp.concatenate([res[:, p].reshape(3 * N, 128) for p in range(3)], axis=1)
    ordered = permuted(phases, inv_ref[...])
    for t in range(3):
        out_ref[t, 0] = ordered[t * N : (t + 1) * N]


def column_tables():
    order = np.zeros((LANES, LANES + 128), np.float32)
    for at in range(LANES):
        order[3 * (at % 128) + at // 128, at] = 1.0
    for at in range(128):
        order[(3 * at - 1) % LANES, LANES + at] = 1.0
    fwd = jnp.asarray(np.concatenate([order, order]), BF16)
    back = order[:, :LANES].T
    inv = jnp.asarray(np.concatenate([back, back]), BF16)
    return fwd, inv


def block(lead, step=0):
    return pl.BlockSpec((lead, 1, N, LANES), lambda l: (step, l, 0, 0))


def whole(shape):
    return pl.BlockSpec(shape, lambda l: (0,) * len(shape))


def phased(*lead):
    shape = lead + (PADDED, 128)
    return pl.BlockSpec(memory_space=pltpu.VMEM), pltpu.VMEM((3,) + shape, F32)


PHASED = [phased(3, 4), phased(2, 4), phased(1, 3)]


def take_columns(sens, zonal, merid, left, right, fwd):
    return pl.pallas_call(
        take,
        grid=(3,),
        in_specs=[block(3), block(2), block(1, 1), whole((N, 128)), whole((N, 128)), whole(fwd.shape)],
        out_specs=[spec for spec, _ in PHASED],
        out_shape=[shape for _, shape in PHASED],
        compiler_params=params(TAKE_MIB),
        cost_estimate=pl.CostEstimate(flops=9 * 10**9, bytes_accessed=26 * 10**6, transcendentals=0),
        name="take",
    )(sens, zonal, merid, left, right, fwd)


def take_column_free(merid, fwd):
    spec, shape = PHASED[2]
    return pl.pallas_call(
        take_alone,
        grid=(3,),
        in_specs=[block(1), whole(fwd.shape)],
        out_specs=spec,
        out_shape=shape,
        compiler_params=params(TAKE_MIB),
        cost_estimate=pl.CostEstimate(flops=10**9, bytes_accessed=4 * 10**6, transcendentals=0),
        name="take_alone",
    )(merid, fwd)


def run_steps(lam, zon, mer, mer_now, a, b, fwd, inv):
    metric = metric_tables()
    rows_msg = pl.BlockSpec((1, 32, LANES), lambda l: (l, 0, 0))
    return pl.pallas_call(
        advance,
        grid=(3,),
        in_specs=[spec for spec, _ in PHASED + PHASED[2:]] + [rows_msg, rows_msg]
        + [whole(fwd.shape), whole(inv.shape), whole(metric.shape)],
        out_specs=block(3),
        out_shape=jax.ShapeDtypeStruct((3, 3, N, N), F32),
        scratch_shapes=[
            pltpu.VMEM((3, 4, 2 * HALO, 8, 128), F32),
            pltpu.VMEM((2, 4, 2 * HALO, 8, 128), F32),
            pltpu.VMEM((2, 3, 2 * HALO, 8, 128), F32),
            pltpu.VMEM((3, 3, ROWS + 6, 8, 128), F32),
            pltpu.VMEM((3, 4, ROWS + 6, 8, 128), F32),
            pltpu.VMEM((3, 3, N, 128), F32),
            pltpu.VMEM((ROWS + 12, 8, 128), F32),
            pltpu.VMEM((ROWS + 12, 8, 128), F32),
        ],
        compiler_params=params(MAIN_MIB),
        name="advance",
    )(lam, zon, mer, mer_now, a, b, fwd, inv, metric)


def exchanges(lat_count, lon_count):
    def at(la, lo):
        return la * lon_count + lo % lon_count

    cells = [(la, lo) for la in range(lat_count) for lo in range(lon_count)]
    half = lon_count // 2
    left = [(at(la, lo), at(la, lo ^ 1)) for la, lo in cells]
    right = [(at(la, lo), at(la, lo + 1 if lo % 2 else lo - 1)) for la, lo in cells]
    a = [(at(la, lo), at(la ^ 1, lo)) for la, lo in cells]
    b = []
    for la, lo in cells:
        to = la + 1 if la % 2 else la - 1
        if to < 0 or to == lat_count:
            b.append((at(la, lo), at(la, lo + half)))
        else:
            b.append((at(la, lo), at(to, lo)))
    return left, right, a, b


def metric_tables():
    lat_count = lax.axis_size("lat")
    total = N * lat_count
    rows = N * np.arange(lat_count)[:, None, None] + ROWS * np.arange(8)[None, :, None] + np.arange(-6, ROWS + 6)
    h = np.abs(np.sin(np.pi * (rows + 0.5) / total))
    g = np.where(rows % total == 0, 0.0, np.abs(np.sin(np.pi * rows / total)))
    table = np.zeros((lat_count, 2, 8, 128), np.float32)
    table[:, 0, :, : ROWS + 12] = 1.0 / h
    table[:, 1, :, : ROWS + 12] = g / 24.0
    return jnp.asarray(table)


def local(sens, zonal, merid):
    lat_count, lon_count = lax.axis_size("lat"), lax.axis_size("lon")
    to_left, to_right, to_a, to_b = exchanges(lat_count, lon_count)
    rims = [(x[:, :, :8], x[:, :, N - 8 :]) for x in (sens, zonal, merid)]
    sens, zonal, merid = [pltpu.with_memory_space_constraint(x, pltpu.HBM) for x in (sens, zonal, merid)]
    fwd, inv = column_tables()
    mer_now = take_column_free(merid, fwd)
    left, right = make_columns_message(sens, zonal, merid)
    left = lax.ppermute(left, AXES, to_left)
    right = lax.ppermute(right, AXES, to_right)
    a, b = make_rows_message(rims, left, right)
    lam, zon, mer = take_columns(sens, zonal, merid, left, right, fwd)
    a = lax.ppermute(a, AXES, to_a)
    b = lax.ppermute(b, AXES, to_b)
    return run_steps(lam, zon, mer, mer_now, a, b, fwd, inv)


def solution(mesh):
    placed = P(None, None, "lat", "lon")
    return jax.shard_map(local, mesh=mesh, in_specs=(placed,) * 3, out_specs=placed, check_vma=False)
```

```python
import jax
import jax.numpy as jnp
import numpy as np
from jax import lax
from jax.experimental import pallas as pl
from jax.experimental.pallas import tpu as pltpu
from jax.sharding import PartitionSpec as P

N = 360
LANES = 384
HALO = 6
ROWS = N // 8
FRONT = 8
TAKE_MIB = 24
MAIN_MIB = 28
PADDED = 384
UNROLL = 9
F32 = jnp.float32
BF16 = jnp.bfloat16
AXES = ("lat", "lon")


def params(mebibytes):
    return pltpu.CompilerParams(vmem_limit_bytes=mebibytes * 2**20)


def lam_base(level, tracer):
    return 6 * (3 * level + tracer)


def z1_base(level):
    return 54 + 6 * level


def m1_base(level):
    return 72 + 3 * level


def z0_base(level):
    return 81 + 3 * level


def pack_columns(sw_ref, se_ref, zw_ref, ze_ref, mw_ref, me_ref, left_ref, right_ref):
    level = pl.program_id(1)
    odd = lax.axis_index("lon") % 2
    jobs = [(sw_ref, se_ref, t, HALO, lam_base(level, t)) for t in range(3)]
    jobs.append((zw_ref, ze_ref, 1, HALO, z1_base(level)))
    jobs.append((mw_ref, me_ref, 0, 3, m1_base(level)))
    jobs.append((zw_ref, ze_ref, 0, 3, z0_base(level)))
    rows = left_ref.shape[0]
    lane = lax.broadcasted_iota(jnp.int32, (rows, 128), 1)
    is_odd = (jnp.zeros((rows, 128), jnp.int32) + odd) == 1
    east = jnp.where(is_odd, right_ref[...], left_ref[...])
    west = jnp.where(is_odd, left_ref[...], right_ref[...])
    for w_ref, e_ref, k, width, base in jobs:
        both = jnp.where(lane < 64, w_ref[k, 0], e_ref[k, 0])
        turned_e = pltpu.roll(both, lax.rem(base + 30 - (HALO - width) + 128, 128), 1)
        turned_w = turned_e if width == HALO else pltpu.roll(both, base + 30, 1)
        east = jnp.where((lane >= base) & (lane < base + width), turned_e, east)
        west = jnp.where((lane >= base + 30) & (lane < base + 30 + width), turned_w, west)
    left_ref[...] = jnp.where(is_odd, west, east)
    right_ref[...] = jnp.where(is_odd, east, west)


def make_columns_message(sens, zonal, merid):
    part = N

    def spec(lead, step, tile):
        return pl.BlockSpec((lead, 1, part, 128), lambda r, l: (step, l, r, tile))

    whole = pl.BlockSpec((part, 128), lambda r, l: (r, 0))
    shape = jax.ShapeDtypeStruct((N, 128), F32)
    return pl.pallas_call(
        pack_columns,
        grid=(N // part, 3),
        in_specs=[spec(3, 0, 0), spec(3, 0, 2), spec(2, 0, 0), spec(2, 0, 2), spec(1, 1, 0), spec(1, 1, 2)],
        out_specs=[whole, whole],
        out_shape=[shape, shape],
        compiler_params=params(24),
        name="pack_columns",
    )(sens, sens, zonal, zonal, merid, merid)


def with_halo(own, east_msg, west_msg, base, width, lane):
    from_west = pltpu.roll(west_msg, (256 - width - base) % 128, 1)
    from_east = pltpu.roll(east_msg, (330 - base) % 128, 1)
    return jnp.where(lane < 104, own, jnp.where(lane < 116, from_east, from_west))


def sorted_by_side(left, right, odd, shape):
    is_odd = (jnp.zeros(shape, jnp.int32) + odd) == 1
    return jnp.where(is_odd, right, left), jnp.where(is_odd, left, right)


def flipped(rows, count):
    return jnp.concatenate([rows[count - 1 - k : count - k] for k in range(count)], axis=0)


def pack_rows(ss_ref, sn_ref, zs_ref, zn_ref, ms_ref, mn_ref, ls_ref, ln_ref, rs_ref, rn_ref, a_ref, b_ref):
    lat = lax.axis_index("lat")
    odd = lax.axis_index("lon") % 2
    lane = lax.broadcasted_iota(jnp.int32, (8, 128), 1)

    def mask(flag):
        return (jnp.zeros((8, 128), jnp.int32) + flag.astype(jnp.int32)) == 1

    turn_south, turn_north = mask(lat == 0), mask(lat == lax.axis_size("lat") - 1)
    lat_odd = mask(lat % 2)
    msgs_south = sorted_by_side(ls_ref[...], rs_ref[...], odd, (8, 128))
    msgs_north = sorted_by_side(ln_ref[...], rn_ref[...], odd, (8, 128))
    for level in range(3):
        slots = [(ss_ref, sn_ref, t, HALO, HALO, lam_base(level, t), 6 * t, 1.0) for t in range(3)]
        slots.append((ms_ref, mn_ref, 1, 6, 3, m1_base(level), 18, -1.0))
        slots.append((zs_ref, zn_ref, 1, 3, HALO, z1_base(level), 24, 1.0))
        slots.append((ms_ref, mn_ref, 0, 3, 0, 0, 27, -1.0))
        for s_ref, n_ref, k, count, width, base, at, sign in slots:
            for tile in range(3):
                cols = slice(tile * 128, (tile + 1) * 128)
                south, north = s_ref[k, level, :, cols], n_ref[k, level, :, cols]
                if tile == 2:
                    if width:
                        south = with_halo(south, *msgs_south, base, width, lane)
                        north = with_halo(north, *msgs_north, base, width, lane)
                    else:
                        south, north = jnp.where(lane < 104, south, 0.0), jnp.where(lane < 104, north, 0.0)
                south, north = south[:count], north[8 - count :]
                south = jnp.where(turn_south[:count], sign * flipped(south, count), south)
                north = jnp.where(turn_north[:count], sign * flipped(north, count), north)
                a_ref[level, pl.ds(at, count), cols] = jnp.where(lat_odd[:count], south, north)
                b_ref[level, pl.ds(at, count), cols] = jnp.where(lat_odd[:count], north, south)
        for out in (a_ref, b_ref):
            out[level, pl.ds(30, 2), :] = jnp.zeros((2, LANES), F32)


def make_rows_message(rims, left, right):
    last = N // 8 - 1

    def spec(lead):
        return pl.BlockSpec((lead, 3, 8, LANES), lambda i: (0, 0, 0, 0))

    def msg(block):
        return pl.BlockSpec((8, 128), lambda i: (block, 0))

    out = pl.BlockSpec((3, 32, LANES), lambda i: (0, 0, 0))
    shape = jax.ShapeDtypeStruct((3, 32, LANES), F32)
    return pl.pallas_call(
        pack_rows,
        grid=(1,),
        in_specs=[spec(3), spec(3), spec(2), spec(2), spec(2), spec(2), msg(0), msg(last), msg(0), msg(last)],
        out_specs=[out, out],
        out_shape=[shape, shape],
        compiler_params=params(24),
        name="pack_rows",
    )(*rims, left, left, right, right)


def permuted(values, table):
    high = values.astype(BF16)
    low = (values - high.astype(F32)).astype(BF16)
    return jnp.dot(jnp.concatenate([high, low], axis=1), table, preferred_element_type=F32)


def weights(total, scale):
    speed = jnp.abs(total) * 0.5
    lead = total * scale
    quad = lead * speed
    b = quad - quad * speed
    a = lead - quad - b
    c = (quad + b + b) * 12.0
    zero = jnp.zeros_like(b)
    return a, jnp.maximum(b, zero), jnp.minimum(b, zero), jnp.maximum(c, zero), jnp.minimum(c, zero)


def y_pass(load, wind, hinv, gface, store, first, last):
    scaled, faces, parts, eps, dee = {}, {}, {}, {}, {}

    def scaled_at(i):
        if i not in scaled:
            h = hinv(i)
            scaled[i] = [load(t, i) * h for t in range(3)]
        return scaled[i]

    def parts_at(f):
        if f not in parts:
            w = weights(wind(f - 1) + wind(f), gface(f))
            lo, hi = scaled_at(f - 1), scaled_at(f)
            phi = [hi[t] - lo[t] for t in range(3)]
            parts[f] = [[x * p for x in w] for p in phi]
        return parts[f]

    def eps_at(f):
        if f not in eps:
            p0, p1, pm = parts_at(f), parts_at(f + 1), parts_at(f - 1)
            eps[f] = [p0[t][0] - p1[t][1] - pm[t][2] for t in range(3)]
        return eps[f]

    def dee_at(i):
        if i not in dee:
            e0, e1 = eps_at(i), eps_at(i + 1)
            dee[i] = [e0[t] + e1[t] for t in range(3)]
        return dee[i]

    for i in range(first, last):
        dm, d0, dp = dee_at(i - 1), dee_at(i), dee_at(i + 1)
        p0, p1 = parts_at(i), parts_at(i + 1)
        for t in range(3):
            store(t, i, load(t, i) + (p0[t][4] + p1[t][3]) + (8.0 * d0[t] - (dm[t] + dp[t])))


def x_row(field, total, acc):
    w = [weights(total[p], 1.0 / 24.0) for p in range(3)]

    def one(f, base):
        phi = [f[0] - f[3], f[1] - f[0], f[2] - f[1]]
        a, bp, bm, cp, cm = [[w[p][k] * phi[p] for p in range(3)] for k in range(5)]
        e0 = a[0] - bp[1] - pltpu.roll(bm[2], 1, 1)
        e1 = a[1] - bp[2] - bm[0]
        e2 = a[2] - pltpu.roll(bp[0], 127, 1) - bm[1]
        s0, s1, s2 = 7.0 * e0, 7.0 * e1, 7.0 * e2
        out0 = (base[0] + cm[0]) + (cp[1] + s0) + (s1 - e2) - pltpu.roll(e2, 1, 1)
        out1 = (base[1] + cm[1]) + (cp[2] + s1) + (s2 - e0) - pltpu.roll(e0, 127, 1)
        out2 = (base[2] + cm[2]) + (s2 - e1) + pltpu.roll(cp[0] + (s0 - e1), 127, 1)
        return out0, out1, out2

    return [one(field[t], acc[t]) for t in range(3)]


def take(s_ref, z_ref, m_ref, left_ref, right_ref, fwd_ref, lam_ref, zon_ref, mer_ref):
    level = pl.program_id(0)
    lane = lax.broadcasted_iota(jnp.int32, (N, 128), 1)
    lon_odd = lax.axis_index("lon") % 2
    east_msg, west_msg = sorted_by_side(left_ref[...], right_ref[...], lon_odd, (N, 128))
    jobs = [(s_ref, lam_ref, [(t, HALO, lam_base(level, t)) for t in range(3)])]
    jobs.append((z_ref, zon_ref, [(1, HALO, z1_base(level)), (0, 3, z0_base(level))]))
    jobs.append((m_ref, mer_ref, [(0, 3, m1_base(level))]))
    for ref, dst, fields in jobs:
        stack = []
        for k, width, base in fields:
            tail = ref[k, 0, :, 256:384]
            tail = with_halo(tail, east_msg, west_msg, base, width, lane)
            stack.append(jnp.concatenate([ref[k, 0, :, 0:256], tail], axis=1))
        count = dst.shape[2]
        moved = permuted(jnp.concatenate(stack, axis=0), fwd_ref[:, : 128 * count])
        for n, (k, _, _) in enumerate(fields):
            for p in range(count):
                dst[level, k, p, pl.ds(FRONT, N), :] = moved[n * N : (n + 1) * N, p * 128 : (p + 1) * 128]


def take_alone(m_ref, fwd_ref, *refs):
    mer_ref = refs[6]

    @pl.when(pl.program_id(0) == 0)
    def _():
        for src, dst in zip(refs[:6], refs[7:]):
            dst[...] = src[...]

    lane = lax.broadcasted_iota(jnp.int32, (N, 128), 1)
    tail = jnp.where(lane < 104, m_ref[0, 0, :, 256:384], 0.0)
    own = jnp.concatenate([m_ref[0, 0, :, 0:256], tail], axis=1)
    moved = permuted(own, fwd_ref[:, :LANES])
    for p in range(3):
        mer_ref[pl.program_id(0), 0, p, pl.ds(FRONT, N), :] = moved[:, p * 128 : (p + 1) * 128]


def advance(
    lam, zon, mer, mer_now, a_ref, b_ref, fwd_ref, inv_ref, metric_ref,
    out_ref, lam_e, zon_e, mer_e, acc, lam1, res, h_ref, g_ref,
):
    level = pl.program_id(0)
    lat_odd = lax.axis_index("lat") % 2
    sublane = lax.broadcasted_iota(jnp.int32, (8, 128), 0)

    @pl.when(level == 0)
    def _():
        both = metric_ref[lax.axis_index("lat")]
        for i in range(ROWS + 12):
            h_ref[i] = jnp.broadcast_to(both[0, :, i : i + 1], (8, 128))
            g_ref[i] = jnp.broadcast_to(both[1, :, i : i + 1], (8, 128))

    def strip(ref, j, p, i):
        return ref[level, j, p, pl.ds(FRONT + i, 8, stride=ROWS), :]

    got_a, got_b = permuted(a_ref[0], fwd_ref[...]), permuted(b_ref[0], fwd_ref[...])
    odd = (jnp.zeros((32, LANES + 128), jnp.int32) + lat_odd) == 1
    north = jnp.where(odd, got_b, got_a)
    south = jnp.where(odd, got_a, got_b)
    slots = [(lam, t, lam_e, t, 6, 6 * t) for t in range(3)]
    slots += [(mer, 0, mer_e, 1, 6, 18), (zon, 1, zon_e, 1, 3, 24), (mer_now, 0, mer_e, 0, 3, 27)]
    for src, k_src, dst, j, count, at in slots:
        for p in range(dst.shape[1]):
            cols = slice(p * 128, (p + 1) * 128)
            for k in range(count):
                low = jnp.broadcast_to(south[at + k : at + k + 1, cols], (8, 128))
                dst[j, p, HALO - count + k] = jnp.where(sublane == 0, low, strip(src, k_src, p, k - count))
                high = jnp.broadcast_to(north[at + k : at + k + 1, cols], (8, 128))
                dst[j, p, HALO + k] = jnp.where(sublane == 7, high, strip(src, k_src, p, ROWS + k))

    def row(ref, edge, j, p, i, k=None):
        if i < 0:
            return edge[j, p, i + HALO]
        if i >= ROWS:
            return edge[j, p, i - ROWS + HALO]
        return strip(ref, j if k is None else k, p, i)

    def hinv(i):
        return h_ref[i + 6]

    def gface(f):
        return g_ref[f + 6]

    def y_one(p, _):
        def store(t, i, value):
            acc[t, p, i + 3] = value

        y_pass(
            lambda t, i: row(lam, lam_e, t, p, i), lambda i: row(mer, mer_e, 1, p, i, 0),
            hinv, gface, store, -3, ROWS + 3,
        )
        return 0

    lax.fori_loop(0, 3, y_one, 0)

    def x_first(i, fetch):
        field = [[fetch(lam, lam_e, t, p, i) for p in range(4)] for t in range(3)]
        z = [fetch(zon, zon_e, 1, p, i) for p in range(4)]
        base = [[acc[t, p, i + 3] for p in range(3)] for t in range(3)]
        new = x_row(field, [z[0] + z[3], z[1] + z[0], z[2] + z[1]], base)
        for t in range(3):
            for p in range(3):
                lam1[t, p, i + 3] = new[t][p]

    for i in (-3, -2, -1, ROWS, ROWS + 1, ROWS + 2):
        x_first(i, row)

    def x_one(q, _):
        for k in range(UNROLL):
            x_first(UNROLL * q + k, lambda ref, edge, j, p, i: strip(ref, j, p, i))
        return 0

    lax.fori_loop(0, ROWS // UNROLL, x_one, 0)

    def y_two(p, _):
        def store(t, i, value):
            acc[t, p, i] = value

        y_pass(
            lambda t, i: lam1[t, p, i + 3], lambda i: row(mer_now, mer_e, 0, p, i),
            hinv, gface, store, 0, ROWS,
        )
        for k in range(ROWS // 3):
            for t in range(3):
                lam1[t, 3, p * (ROWS // 3) + k + 3] = pltpu.roll(lam1[t, 2, p * (ROWS // 3) + k + 3], 1, 1)
        return 0

    lax.fori_loop(0, 3, y_two, 0)

    def x_two(q, _):
        for k in range(UNROLL):
            i = UNROLL * q + k
            field = [[lam1[t, p, i + 3] for p in range(4)] for t in range(3)]
            z = [strip(zon, 0, p, i) for p in range(4)]
            base = [[acc[t, p, i] for p in range(3)] for t in range(3)]
            new = x_row(field, [z[0] + z[3], z[1] + z[0], z[2] + z[1]], base)
            for t in range(3):
                for p in range(3):
                    res[t, p, pl.ds(i, 8, stride=ROWS), :] = new[t][p]
        return 0

    lax.fori_loop(0, ROWS // UNROLL, x_two, 0)

    phases = jnp.concatenate([res[:, p].reshape(3 * N, 128) for p in range(3)], axis=1)
    ordered = permuted(phases, inv_ref[...])
    for t in range(3):
        out_ref[t, 0] = ordered[t * N : (t + 1) * N]


def column_tables():
    order = np.zeros((LANES, LANES + 128), np.float32)
    for at in range(LANES):
        order[3 * (at % 128) + at // 128, at] = 1.0
    for at in range(128):
        order[(3 * at - 1) % LANES, LANES + at] = 1.0
    fwd = jnp.asarray(np.concatenate([order, order]), BF16)
    back = order[:, :LANES].T
    inv = jnp.asarray(np.concatenate([back, back]), BF16)
    return fwd, inv


def block(lead, step=0):
    return pl.BlockSpec((lead, 1, N, LANES), lambda l: (step, l, 0, 0))


def whole(shape):
    return pl.BlockSpec(shape, lambda l: (0,) * len(shape))


def phased(*lead):
    shape = lead + (PADDED, 128)
    return pl.BlockSpec(memory_space=pltpu.VMEM), pltpu.VMEM((3,) + shape, F32)


PHASED = [phased(3, 4), phased(2, 4), phased(1, 3)]


def take_columns(sens, zonal, merid, left, right, fwd):
    return pl.pallas_call(
        take,
        grid=(3,),
        in_specs=[block(3), block(2), block(1, 1), whole((N, 128)), whole((N, 128)), whole(fwd.shape)],
        out_specs=[spec for spec, _ in PHASED],
        out_shape=[shape for _, shape in PHASED],
        compiler_params=params(TAKE_MIB),
        cost_estimate=pl.CostEstimate(flops=9 * 10**9, bytes_accessed=26 * 10**6, transcendentals=0),
        name="take",
    )(sens, zonal, merid, left, right, fwd)


def take_column_free(sens, zonal, merid, fwd):
    spec, shape = PHASED[2]
    arrays = [(sens, 3), (zonal, 2), (merid, 2)]

    def rim(lead, at):
        return pl.BlockSpec((lead, 3, 8, LANES), lambda l: (0, 0, at, 0))

    near = pl.BlockSpec(memory_space=pltpu.VMEM)
    return pl.pallas_call(
        take_alone,
        grid=(3,),
        in_specs=[block(1), whole(fwd.shape)] + [rim(lead, at) for _, lead in arrays for at in (0, N // 8 - 1)],
        out_specs=[spec] + [near] * 6,
        out_shape=[shape] + [pltpu.VMEM((lead, 3, 8, LANES), F32) for _, lead in arrays for _ in range(2)],
        compiler_params=params(TAKE_MIB),
        cost_estimate=pl.CostEstimate(flops=10**9, bytes_accessed=4 * 10**6, transcendentals=0),
        name="take_alone",
    )(merid, fwd, *(x for x, _ in arrays for _ in range(2)))


def run_steps(lam, zon, mer, mer_now, a, b, fwd, inv):
    metric = metric_tables()
    rows_msg = pl.BlockSpec((1, 32, LANES), lambda l: (l, 0, 0))
    return pl.pallas_call(
        advance,
        grid=(3,),
        in_specs=[spec for spec, _ in PHASED + PHASED[2:]] + [rows_msg, rows_msg]
        + [whole(fwd.shape), whole(inv.shape), whole(metric.shape)],
        out_specs=block(3),
        out_shape=jax.ShapeDtypeStruct((3, 3, N, N), F32),
        scratch_shapes=[
            pltpu.VMEM((3, 4, 2 * HALO, 8, 128), F32),
            pltpu.VMEM((2, 4, 2 * HALO, 8, 128), F32),
            pltpu.VMEM((2, 3, 2 * HALO, 8, 128), F32),
            pltpu.VMEM((3, 3, ROWS + 6, 8, 128), F32),
            pltpu.VMEM((3, 4, ROWS + 6, 8, 128), F32),
            pltpu.VMEM((3, 3, N, 128), F32),
            pltpu.VMEM((ROWS + 12, 8, 128), F32),
            pltpu.VMEM((ROWS + 12, 8, 128), F32),
        ],
        compiler_params=params(MAIN_MIB),
        name="advance",
    )(lam, zon, mer, mer_now, a, b, fwd, inv, metric)


def exchanges(lat_count, lon_count):
    def at(la, lo):
        return la * lon_count + lo % lon_count

    cells = [(la, lo) for la in range(lat_count) for lo in range(lon_count)]
    half = lon_count // 2
    left = [(at(la, lo), at(la, lo ^ 1)) for la, lo in cells]
    right = [(at(la, lo), at(la, lo + 1 if lo % 2 else lo - 1)) for la, lo in cells]
    a = [(at(la, lo), at(la ^ 1, lo)) for la, lo in cells]
    b = []
    for la, lo in cells:
        to = la + 1 if la % 2 else la - 1
        if to < 0 or to == lat_count:
            b.append((at(la, lo), at(la, lo + half)))
        else:
            b.append((at(la, lo), at(to, lo)))
    return left, right, a, b


def metric_tables():
    lat_count = lax.axis_size("lat")
    total = N * lat_count
    rows = N * np.arange(lat_count)[:, None, None] + ROWS * np.arange(8)[None, :, None] + np.arange(-6, ROWS + 6)
    h = np.abs(np.sin(np.pi * (rows + 0.5) / total))
    g = np.where(rows % total == 0, 0.0, np.abs(np.sin(np.pi * rows / total)))
    table = np.zeros((lat_count, 2, 8, 128), np.float32)
    table[:, 0, :, : ROWS + 12] = 1.0 / h
    table[:, 1, :, : ROWS + 12] = g / 24.0
    return jnp.asarray(table)


def local(sens, zonal, merid):
    lat_count, lon_count = lax.axis_size("lat"), lax.axis_size("lon")
    to_left, to_right, to_a, to_b = exchanges(lat_count, lon_count)
    sens, zonal, merid = [pltpu.with_memory_space_constraint(x, pltpu.HBM) for x in (sens, zonal, merid)]
    fwd, inv = column_tables()
    mer_now, *rims = take_column_free(sens, zonal, merid, fwd)
    left, right = make_columns_message(sens, zonal, merid)
    left = lax.ppermute(left, AXES, to_left)
    right = lax.ppermute(right, AXES, to_right)
    a, b = make_rows_message(rims, left, right)
    lam, zon, mer = take_columns(sens, zonal, merid, left, right, fwd)
    a = lax.ppermute(a, AXES, to_a)
    b = lax.ppermute(b, AXES, to_b)
    return run_steps(lam, zon, mer, mer_now, a, b, fwd, inv)


def solution(mesh):
    placed = P(None, None, "lat", "lon")
    return jax.shard_map(local, mesh=mesh, in_specs=(placed,) * 3, out_specs=placed, check_vma=False)
```

```python
import jax
import jax.numpy as jnp
import numpy as np
from jax import lax
from jax.experimental import pallas as pl
from jax.experimental.pallas import tpu as pltpu
from jax.sharding import PartitionSpec as P

N = 360
LANES = 384
HALO = 6
ROWS = N // 8
FRONT = 8
TAKE_MIB = 24
MAIN_MIB = 28
PADDED = 384
UNROLL = 9
F32 = jnp.float32
BF16 = jnp.bfloat16
AXES = ("lat", "lon")


def params(mebibytes):
    return pltpu.CompilerParams(vmem_limit_bytes=mebibytes * 2**20)


def lam_base(level, tracer):
    return 6 * (3 * level + tracer)


def z1_base(level):
    return 54 + 6 * level


def m1_base(level):
    return 72 + 3 * level


def z0_base(level):
    return 81 + 3 * level


def pack_columns(sw_ref, se_ref, zw_ref, ze_ref, mw_ref, me_ref, left_ref, right_ref):
    level = pl.program_id(1)
    odd = lax.axis_index("lon") % 2
    jobs = [(sw_ref, se_ref, t, HALO, lam_base(level, t)) for t in range(3)]
    jobs.append((zw_ref, ze_ref, 1, HALO, z1_base(level)))
    jobs.append((mw_ref, me_ref, 0, 3, m1_base(level)))
    jobs.append((zw_ref, ze_ref, 0, 3, z0_base(level)))
    rows = left_ref.shape[0]
    lane = lax.broadcasted_iota(jnp.int32, (rows, 128), 1)
    is_odd = (jnp.zeros((rows, 128), jnp.int32) + odd) == 1
    east = jnp.where(is_odd, right_ref[...], left_ref[...])
    west = jnp.where(is_odd, left_ref[...], right_ref[...])
    for w_ref, e_ref, k, width, base in jobs:
        both = jnp.where(lane < 64, w_ref[k, 0], e_ref[k, 0])
        turned_e = pltpu.roll(both, lax.rem(base + 30 - (HALO - width) + 128, 128), 1)
        turned_w = turned_e if width == HALO else pltpu.roll(both, base + 30, 1)
        east = jnp.where((lane >= base) & (lane < base + width), turned_e, east)
        west = jnp.where((lane >= base + 30) & (lane < base + 30 + width), turned_w, west)
    left_ref[...] = jnp.where(is_odd, west, east)
    right_ref[...] = jnp.where(is_odd, east, west)


def make_columns_message(sens, zonal, merid):
    part = N

    def spec(lead, step, tile):
        return pl.BlockSpec((lead, 1, part, 128), lambda r, l: (step, l, r, tile))

    whole = pl.BlockSpec((part, 128), lambda r, l: (r, 0))
    shape = jax.ShapeDtypeStruct((N, 128), F32)
    return pl.pallas_call(
        pack_columns,
        grid=(N // part, 3),
        in_specs=[spec(3, 0, 0), spec(3, 0, 2), spec(2, 0, 0), spec(2, 0, 2), spec(1, 1, 0), spec(1, 1, 2)],
        out_specs=[whole, whole],
        out_shape=[shape, shape],
        compiler_params=params(24),
        name="pack_columns",
    )(sens, sens, zonal, zonal, merid, merid)


def with_halo(own, east_msg, west_msg, base, width, lane):
    from_west = pltpu.roll(west_msg, (256 - width - base) % 128, 1)
    from_east = pltpu.roll(east_msg, (330 - base) % 128, 1)
    return jnp.where(lane < 104, own, jnp.where(lane < 116, from_east, from_west))


def sorted_by_side(left, right, odd, shape):
    is_odd = (jnp.zeros(shape, jnp.int32) + odd) == 1
    return jnp.where(is_odd, right, left), jnp.where(is_odd, left, right)


def flipped(rows, count):
    return jnp.concatenate([rows[count - 1 - k : count - k] for k in range(count)], axis=0)


def pack_rows(ss_ref, sn_ref, zs_ref, zn_ref, ms_ref, mn_ref, ls_ref, ln_ref, rs_ref, rn_ref, a_ref, b_ref):
    lat = lax.axis_index("lat")
    odd = lax.axis_index("lon") % 2
    lane = lax.broadcasted_iota(jnp.int32, (8, 128), 1)

    def mask(flag):
        return (jnp.zeros((8, 128), jnp.int32) + flag.astype(jnp.int32)) == 1

    turn_south, turn_north = mask(lat == 0), mask(lat == lax.axis_size("lat") - 1)
    lat_odd = mask(lat % 2)
    msgs_south = sorted_by_side(ls_ref[...], rs_ref[...], odd, (8, 128))
    msgs_north = sorted_by_side(ln_ref[...], rn_ref[...], odd, (8, 128))
    for level in range(3):
        slots = [(ss_ref, sn_ref, t, HALO, HALO, lam_base(level, t), 6 * t, 1.0) for t in range(3)]
        slots.append((ms_ref, mn_ref, 1, 6, 3, m1_base(level), 18, -1.0))
        slots.append((zs_ref, zn_ref, 1, 3, HALO, z1_base(level), 24, 1.0))
        slots.append((ms_ref, mn_ref, 0, 3, 0, 0, 27, -1.0))
        for s_ref, n_ref, k, count, width, base, at, sign in slots:
            for tile in range(3):
                cols = slice(tile * 128, (tile + 1) * 128)
                south, north = s_ref[k, level, :, cols], n_ref[k, level, :, cols]
                if tile == 2:
                    if width:
                        south = with_halo(south, *msgs_south, base, width, lane)
                        north = with_halo(north, *msgs_north, base, width, lane)
                    else:
                        south, north = jnp.where(lane < 104, south, 0.0), jnp.where(lane < 104, north, 0.0)
                south, north = south[:count], north[8 - count :]
                south = jnp.where(turn_south[:count], sign * flipped(south, count), south)
                north = jnp.where(turn_north[:count], sign * flipped(north, count), north)
                a_ref[level, pl.ds(at, count), cols] = jnp.where(lat_odd[:count], south, north)
                b_ref[level, pl.ds(at, count), cols] = jnp.where(lat_odd[:count], north, south)
        for out in (a_ref, b_ref):
            out[level, pl.ds(30, 2), :] = jnp.zeros((2, LANES), F32)


def make_rows_message(rims, left, right):
    last = N // 8 - 1

    def spec(lead):
        return pl.BlockSpec((lead, 3, 8, LANES), lambda i: (0, 0, 0, 0))

    def msg(block):
        return pl.BlockSpec((8, 128), lambda i: (block, 0))

    out = pl.BlockSpec((3, 32, LANES), lambda i: (0, 0, 0))
    shape = jax.ShapeDtypeStruct((3, 32, LANES), F32)
    return pl.pallas_call(
        pack_rows,
        grid=(1,),
        in_specs=[spec(3), spec(3), spec(2), spec(2), spec(2), spec(2), msg(0), msg(last), msg(0), msg(last)],
        out_specs=[out, out],
        out_shape=[shape, shape],
        compiler_params=params(24),
        name="pack_rows",
    )(*rims, left, left, right, right)


def permuted(values, table):
    high = values.astype(BF16)
    low = (values - high.astype(F32)).astype(BF16)
    return jnp.dot(jnp.concatenate([high, low], axis=1), table, preferred_element_type=F32)


def weights(total, scale):
    speed = jnp.abs(total)
    lead = total * scale
    quad = lead * speed
    b = quad - quad * speed
    a = lead - quad - b
    c = (quad + b + b) * 12.0
    zero = jnp.zeros_like(b)
    return a, jnp.maximum(b, zero), jnp.minimum(b, zero), jnp.maximum(c, zero), jnp.minimum(c, zero)


def y_pass(load, wind, hinv, gface, store, first, last):
    scaled, faces, parts, eps, dee = {}, {}, {}, {}, {}

    def scaled_at(i):
        if i not in scaled:
            h = hinv(i)
            scaled[i] = [load(t, i) * h for t in range(3)]
        return scaled[i]

    def parts_at(f):
        if f not in parts:
            w = weights(wind(f - 1) + wind(f), gface(f))
            lo, hi = scaled_at(f - 1), scaled_at(f)
            phi = [hi[t] - lo[t] for t in range(3)]
            parts[f] = [[x * p for x in w] for p in phi]
        return parts[f]

    def eps_at(f):
        if f not in eps:
            p0, p1, pm = parts_at(f), parts_at(f + 1), parts_at(f - 1)
            eps[f] = [p0[t][0] - p1[t][1] - pm[t][2] for t in range(3)]
        return eps[f]

    def dee_at(i):
        if i not in dee:
            e0, e1 = eps_at(i), eps_at(i + 1)
            dee[i] = [e0[t] + e1[t] for t in range(3)]
        return dee[i]

    for i in range(first, last):
        dm, d0, dp = dee_at(i - 1), dee_at(i), dee_at(i + 1)
        p0, p1 = parts_at(i), parts_at(i + 1)
        for t in range(3):
            store(t, i, load(t, i) + (p0[t][4] + p1[t][3]) + (8.0 * d0[t] - (dm[t] + dp[t])))


def x_row(field, total, acc):
    w = [weights(total[p], 1.0 / 12.0) for p in range(3)]

    def one(f, base):
        phi = [f[0] - f[3], f[1] - f[0], f[2] - f[1]]
        a, bp, bm, cp, cm = [[w[p][k] * phi[p] for p in range(3)] for k in range(5)]
        e0 = a[0] - bp[1] - pltpu.roll(bm[2], 1, 1)
        e1 = a[1] - bp[2] - bm[0]
        e2 = a[2] - pltpu.roll(bp[0], 127, 1) - bm[1]
        s0, s1, s2 = 7.0 * e0, 7.0 * e1, 7.0 * e2
        out0 = (base[0] + cm[0]) + (cp[1] + s0) + (s1 - e2) - pltpu.roll(e2, 1, 1)
        out1 = (base[1] + cm[1]) + (cp[2] + s1) + (s2 - e0) - pltpu.roll(e0, 127, 1)
        out2 = (base[2] + cm[2]) + (s2 - e1) + pltpu.roll(cp[0] + (s0 - e1), 127, 1)
        return out0, out1, out2

    return [one(field[t], acc[t]) for t in range(3)]


def take(s_ref, z_ref, m_ref, left_ref, right_ref, fwd_ref, half_ref, lam_ref, zon_ref, mer_ref):
    level = pl.program_id(0)
    lane = lax.broadcasted_iota(jnp.int32, (N, 128), 1)
    lon_odd = lax.axis_index("lon") % 2
    east_msg, west_msg = sorted_by_side(left_ref[...], right_ref[...], lon_odd, (N, 128))
    jobs = [(s_ref, lam_ref, [(t, HALO, lam_base(level, t)) for t in range(3)])]
    jobs.append((z_ref, zon_ref, [(1, HALO, z1_base(level)), (0, 3, z0_base(level))]))
    jobs.append((m_ref, mer_ref, [(0, 3, m1_base(level))]))
    for ref, dst, fields in jobs:
        stack = []
        for k, width, base in fields:
            tail = ref[k, 0, :, 256:384]
            tail = with_halo(tail, east_msg, west_msg, base, width, lane)
            stack.append(jnp.concatenate([ref[k, 0, :, 0:256], tail], axis=1))
        count = dst.shape[2]
        table = fwd_ref if dst is lam_ref else half_ref
        moved = permuted(jnp.concatenate(stack, axis=0), table[:, : 128 * count])
        for n, (k, _, _) in enumerate(fields):
            for p in range(count):
                dst[level, k, p, pl.ds(FRONT, N), :] = moved[n * N : (n + 1) * N, p * 128 : (p + 1) * 128]


def take_alone(m_ref, fwd_ref, *refs):
    mer_ref = refs[6]

    @pl.when(pl.program_id(0) == 0)
    def _():
        for src, dst in zip(refs[:6], refs[7:]):
            dst[...] = src[...]

    lane = lax.broadcasted_iota(jnp.int32, (N, 128), 1)
    tail = jnp.where(lane < 104, m_ref[0, 0, :, 256:384], 0.0)
    own = jnp.concatenate([m_ref[0, 0, :, 0:256], tail], axis=1)
    moved = permuted(own, fwd_ref[:, :LANES])
    for p in range(3):
        mer_ref[pl.program_id(0), 0, p, pl.ds(FRONT, N), :] = moved[:, p * 128 : (p + 1) * 128]


def advance(
    lam, zon, mer, mer_now, a_ref, b_ref, fwd_ref, inv_ref, metric_ref,
    out_ref, lam_e, zon_e, mer_e, acc, lam1, res, h_ref, g_ref,
):
    level = pl.program_id(0)
    lat_odd = lax.axis_index("lat") % 2
    sublane = lax.broadcasted_iota(jnp.int32, (8, 128), 0)

    @pl.when(level == 0)
    def _():
        both = metric_ref[lax.axis_index("lat")]
        for i in range(ROWS + 12):
            h_ref[i] = jnp.broadcast_to(both[0, :, i : i + 1], (8, 128))
            g_ref[i] = jnp.broadcast_to(both[1, :, i : i + 1], (8, 128))

    def strip(ref, j, p, i):
        return ref[level, j, p, pl.ds(FRONT + i, 8, stride=ROWS), :]

    got_a, got_b = permuted(a_ref[0], fwd_ref[...]), permuted(b_ref[0], fwd_ref[...])
    odd = (jnp.zeros((32, LANES + 128), jnp.int32) + lat_odd) == 1
    north = jnp.where(odd, got_b, got_a)
    south = jnp.where(odd, got_a, got_b)
    wind = lax.broadcasted_iota(jnp.int32, (32, LANES + 128), 0) >= 18
    north = jnp.where(wind, 0.5 * north, north)
    south = jnp.where(wind, 0.5 * south, south)
    slots = [(lam, t, lam_e, t, 6, 6 * t) for t in range(3)]
    slots += [(mer, 0, mer_e, 1, 6, 18), (zon, 1, zon_e, 1, 3, 24), (mer_now, 0, mer_e, 0, 3, 27)]
    for src, k_src, dst, j, count, at in slots:
        for p in range(dst.shape[1]):
            cols = slice(p * 128, (p + 1) * 128)
            for k in range(count):
                low = jnp.broadcast_to(south[at + k : at + k + 1, cols], (8, 128))
                dst[j, p, HALO - count + k] = jnp.where(sublane == 0, low, strip(src, k_src, p, k - count))
                high = jnp.broadcast_to(north[at + k : at + k + 1, cols], (8, 128))
                dst[j, p, HALO + k] = jnp.where(sublane == 7, high, strip(src, k_src, p, ROWS + k))

    def row(ref, edge, j, p, i, k=None):
        if i < 0:
            return edge[j, p, i + HALO]
        if i >= ROWS:
            return edge[j, p, i - ROWS + HALO]
        return strip(ref, j if k is None else k, p, i)

    def hinv(i):
        return h_ref[i + 6]

    def gface(f):
        return g_ref[f + 6]

    def y_one(p, _):
        def store(t, i, value):
            acc[t, p, i + 3] = value

        y_pass(
            lambda t, i: row(lam, lam_e, t, p, i), lambda i: row(mer, mer_e, 1, p, i, 0),
            hinv, gface, store, -3, ROWS + 3,
        )
        return 0

    lax.fori_loop(0, 3, y_one, 0)

    def x_first(i, fetch):
        field = [[fetch(lam, lam_e, t, p, i) for p in range(4)] for t in range(3)]
        z = [fetch(zon, zon_e, 1, p, i) for p in range(4)]
        base = [[acc[t, p, i + 3] for p in range(3)] for t in range(3)]
        new = x_row(field, [z[0] + z[3], z[1] + z[0], z[2] + z[1]], base)
        for t in range(3):
            for p in range(3):
                lam1[t, p, i + 3] = new[t][p]

    for i in (-3, -2, -1, ROWS, ROWS + 1, ROWS + 2):
        x_first(i, row)

    def x_one(q, _):
        for k in range(UNROLL):
            x_first(UNROLL * q + k, lambda ref, edge, j, p, i: strip(ref, j, p, i))
        return 0

    lax.fori_loop(0, ROWS // UNROLL, x_one, 0)

    def y_two(p, _):
        def store(t, i, value):
            acc[t, p, i] = value

        y_pass(
            lambda t, i: lam1[t, p, i + 3], lambda i: row(mer_now, mer_e, 0, p, i),
            hinv, gface, store, 0, ROWS,
        )
        for k in range(ROWS // 3):
            for t in range(3):
                lam1[t, 3, p * (ROWS // 3) + k + 3] = pltpu.roll(lam1[t, 2, p * (ROWS // 3) + k + 3], 1, 1)
        return 0

    lax.fori_loop(0, 3, y_two, 0)

    def x_two(q, _):
        for k in range(UNROLL):
            i = UNROLL * q + k
            field = [[lam1[t, p, i + 3] for p in range(4)] for t in range(3)]
            z = [strip(zon, 0, p, i) for p in range(4)]
            base = [[acc[t, p, i] for p in range(3)] for t in range(3)]
            new = x_row(field, [z[0] + z[3], z[1] + z[0], z[2] + z[1]], base)
            for t in range(3):
                for p in range(3):
                    res[t, p, pl.ds(i, 8, stride=ROWS), :] = new[t][p]
        return 0

    lax.fori_loop(0, ROWS // UNROLL, x_two, 0)

    phases = jnp.concatenate([res[:, p].reshape(3 * N, 128) for p in range(3)], axis=1)
    ordered = permuted(phases, inv_ref[...])
    for t in range(3):
        out_ref[t, 0] = ordered[t * N : (t + 1) * N]


def column_tables():
    order = np.zeros((LANES, LANES + 128), np.float32)
    for at in range(LANES):
        order[3 * (at % 128) + at // 128, at] = 1.0
    for at in range(128):
        order[(3 * at - 1) % LANES, LANES + at] = 1.0
    fwd = jnp.asarray(np.concatenate([order, order]), BF16)
    back = order[:, :LANES].T
    inv = jnp.asarray(np.concatenate([back, back]), BF16)
    half = jnp.asarray(0.5 * np.concatenate([order, order]), BF16)
    return fwd, half, inv


def block(lead, step=0):
    return pl.BlockSpec((lead, 1, N, LANES), lambda l: (step, l, 0, 0))


def whole(shape):
    return pl.BlockSpec(shape, lambda l: (0,) * len(shape))


def phased(*lead):
    shape = lead + (PADDED, 128)
    return pl.BlockSpec(memory_space=pltpu.VMEM), pltpu.VMEM((3,) + shape, F32)


PHASED = [phased(3, 4), phased(2, 4), phased(1, 3)]


def take_columns(sens, zonal, merid, left, right, fwd, half):
    return pl.pallas_call(
        take,
        grid=(3,),
        in_specs=[block(3), block(2), block(1, 1), whole((N, 128)), whole((N, 128)), whole(fwd.shape), whole(fwd.shape)],
        out_specs=[spec for spec, _ in PHASED],
        out_shape=[shape for _, shape in PHASED],
        compiler_params=params(TAKE_MIB),
        cost_estimate=pl.CostEstimate(flops=9 * 10**9, bytes_accessed=26 * 10**6, transcendentals=0),
        name="take",
    )(sens, zonal, merid, left, right, fwd, half)


def take_column_free(sens, zonal, merid, fwd):
    spec, shape = PHASED[2]
    arrays = [(sens, 3), (zonal, 2), (merid, 2)]

    def rim(lead, at):
        return pl.BlockSpec((lead, 3, 8, LANES), lambda l: (0, 0, at, 0))

    near = pl.BlockSpec(memory_space=pltpu.VMEM)
    return pl.pallas_call(
        take_alone,
        grid=(3,),
        in_specs=[block(1), whole(fwd.shape)] + [rim(lead, at) for _, lead in arrays for at in (0, N // 8 - 1)],
        out_specs=[spec] + [near] * 6,
        out_shape=[shape] + [pltpu.VMEM((lead, 3, 8, LANES), F32) for _, lead in arrays for _ in range(2)],
        compiler_params=params(TAKE_MIB),
        cost_estimate=pl.CostEstimate(flops=10**9, bytes_accessed=4 * 10**6, transcendentals=0),
        name="take_alone",
    )(merid, fwd, *(x for x, _ in arrays for _ in range(2)))


def run_steps(lam, zon, mer, mer_now, a, b, fwd, inv):
    metric = metric_tables()
    rows_msg = pl.BlockSpec((1, 32, LANES), lambda l: (l, 0, 0))
    return pl.pallas_call(
        advance,
        grid=(3,),
        in_specs=[spec for spec, _ in PHASED + PHASED[2:]] + [rows_msg, rows_msg]
        + [whole(fwd.shape), whole(inv.shape), whole(metric.shape)],
        out_specs=block(3),
        out_shape=jax.ShapeDtypeStruct((3, 3, N, N), F32),
        scratch_shapes=[
            pltpu.VMEM((3, 4, 2 * HALO, 8, 128), F32),
            pltpu.VMEM((2, 4, 2 * HALO, 8, 128), F32),
            pltpu.VMEM((2, 3, 2 * HALO, 8, 128), F32),
            pltpu.VMEM((3, 3, ROWS + 6, 8, 128), F32),
            pltpu.VMEM((3, 4, ROWS + 6, 8, 128), F32),
            pltpu.VMEM((3, 3, N, 128), F32),
            pltpu.VMEM((ROWS + 12, 8, 128), F32),
            pltpu.VMEM((ROWS + 12, 8, 128), F32),
        ],
        compiler_params=params(MAIN_MIB),
        name="advance",
    )(lam, zon, mer, mer_now, a, b, fwd, inv, metric)


def exchanges(lat_count, lon_count):
    def at(la, lo):
        return la * lon_count + lo % lon_count

    cells = [(la, lo) for la in range(lat_count) for lo in range(lon_count)]
    half = lon_count // 2
    left = [(at(la, lo), at(la, lo ^ 1)) for la, lo in cells]
    right = [(at(la, lo), at(la, lo + 1 if lo % 2 else lo - 1)) for la, lo in cells]
    a = [(at(la, lo), at(la ^ 1, lo)) for la, lo in cells]
    b = []
    for la, lo in cells:
        to = la + 1 if la % 2 else la - 1
        if to < 0 or to == lat_count:
            b.append((at(la, lo), at(la, lo + half)))
        else:
            b.append((at(la, lo), at(to, lo)))
    return left, right, a, b


def metric_tables():
    lat_count = lax.axis_size("lat")
    total = N * lat_count
    rows = N * np.arange(lat_count)[:, None, None] + ROWS * np.arange(8)[None, :, None] + np.arange(-6, ROWS + 6)
    h = np.abs(np.sin(np.pi * (rows + 0.5) / total))
    g = np.where(rows % total == 0, 0.0, np.abs(np.sin(np.pi * rows / total)))
    table = np.zeros((lat_count, 2, 8, 128), np.float32)
    table[:, 0, :, : ROWS + 12] = 1.0 / h
    table[:, 1, :, : ROWS + 12] = g / 12.0
    return jnp.asarray(table)


def local(sens, zonal, merid):
    lat_count, lon_count = lax.axis_size("lat"), lax.axis_size("lon")
    to_left, to_right, to_a, to_b = exchanges(lat_count, lon_count)
    sens, zonal, merid = [pltpu.with_memory_space_constraint(x, pltpu.HBM) for x in (sens, zonal, merid)]
    fwd, half, inv = column_tables()
    mer_now, *rims = take_column_free(sens, zonal, merid, half)
    left, right = make_columns_message(sens, zonal, merid)
    left = lax.ppermute(left, AXES, to_left)
    right = lax.ppermute(right, AXES, to_right)
    a, b = make_rows_message(rims, left, right)
    lam, zon, mer = take_columns(sens, zonal, merid, left, right, fwd, half)
    a = lax.ppermute(a, AXES, to_a)
    b = lax.ppermute(b, AXES, to_b)
    return run_steps(lam, zon, mer, mer_now, a, b, fwd, inv)


def solution(mesh):
    placed = P(None, None, "lat", "lon")
    return jax.shard_map(local, mesh=mesh, in_specs=(placed,) * 3, out_specs=placed, check_vma=False)
```
